32 devices in a mesh: grp: 4 (over z), dev: 8 (over y, x, core).
Axes of the slice: x: 2, y: 2, z: 4, core: 2. Of those that a mesh axis runs over, the one named last changes fastest.
Arguments:
- orbitals: bfloat16 [64, 48, 2304], P(('grp', 'dev')), may hold values from -6 to 6
- offsets: int32 [64, 3], P(('grp', 'dev')), may hold values from 0 to 23
- pick: int32 [4, 8, 4], P('grp'), may hold values from 0 to 1
- pair_local: int32 [4, 8, 2], P('grp', 'dev'), may hold values from 0 to 1
- pair_source: int32 [4, 8, 2], P('grp', 'dev'), may hold values from 0 to 3, as said below
- pair_count: int32 [4, 8, 1], P('grp', 'dev'), may hold values from 1 to 2, as said below
Outputs:
- exchange_action: float32 [64, 110592], P('grp', 'dev')
The draws below stay inside these ranges and needn't reach their ends.
Inputs may be any that keep to these rules, and one draw needn't show every extreme that they name: pair_source[g, d, p] is never g; the two slots of one device's list name different groups. Only the first pair_count[g, d, 0] slots of a device's lists are pairs; some device lists exactly 2.
All inputs are finite; a program needn't handle non-finite values.
Results may differ from the reference program's by a relative error of at most 0.002.
Values may be sent and summed in bfloat16 or wider, within the bound.
No kernel may reach another device: no remote copies, remote signals or barrier semaphores. Data moves between devices by JAX's collectives and lax.ppermute only.
A program may use at most 64 MiB of HBM per device.

```python
import math
import jax
import jax.numpy as jnp
from jax import lax

BOX = 48
ORB_DEV = 2
PAIRS = 2
ORBITALS = 64
N_GRP = 4
N_DEV = 8


def draw_pair_source(key, part):
    start = jax.random.randint(jax.random.fold_in(key, 11), (N_GRP, N_DEV, 1), 0, N_GRP - 1)
    slot_index = jnp.arange(PAIRS, dtype=jnp.int32)[None, None, :]
    stride = 1 + (start + slot_index) % (N_GRP - 1)
    own_group = jnp.arange(N_GRP, dtype=jnp.int32)[:, None, None]
    return ((own_group + stride) % N_GRP).astype(jnp.int32)


def draw_pair_count(key, part):
    first_key = jax.random.fold_in(key, 23)
    second_key = jax.random.fold_in(key, 29)
    lowest = PAIRS // 2
    counted = jax.random.randint(first_key, (N_GRP, N_DEV, 1), lowest, PAIRS + 1)
    chosen = jax.random.randint(second_key, (), 0, N_GRP * N_DEV)
    flat_place = jnp.arange(N_GRP * N_DEV, dtype=jnp.int32).reshape(N_GRP, N_DEV, 1)
    return jnp.where(flat_place == chosen, PAIRS, counted).astype(jnp.int32)


def touch_ends(array, key, least, top_value):
    spot = [jax.random.randint(jax.random.fold_in(key, axis), (), 0, length) for axis, length in enumerate(array.shape)]
    main_axis = array.shape.index(max(array.shape))
    beside = spot[:main_axis] + [(spot[main_axis] + 1) % array.shape[main_axis]] + spot[main_axis + 1:]
    return array.at[tuple(spot)].set(least).at[tuple(beside)].set(top_value)


def steps_of(rng, extent, shards, low, high):
    def one(axis_at, shards_of):
        steps = jax.random.uniform(jax.random.fold_in(jax.random.fold_in(rng, 6), axis_at), (shards_of,), jnp.float32, low / len(shards), high / len(shards))
        return jnp.repeat(jnp.exp(steps), extent[axis_at] // shards_of).reshape((-1,) + (1,) * (len(extent) - axis_at - 1))

    factor_of = one(*shards[0])
    for cut in shards[1:]:
        factor_of = factor_of * one(*cut)
    return factor_of


def centred(rng, extent, deviation, most, cuts=(), kind=jnp.bfloat16):
    values = jax.random.normal(rng, extent, jnp.float32) * deviation
    if len(cuts) > 0:
        values = steps_of(rng, extent, cuts, -0.22, 0.18) * values
    return jnp.clip(values, min=-most, max=most).astype(kind)


def setup_inputs(seed: int = 0) -> dict:
    streams_of = jax.random.split(jax.random.key(seed), 7)
    return {
        "orbitals": centred(streams_of[0], (ORBITALS, BOX, BOX * BOX), 1.0, 6.0, ((0, 32),)),
        "offsets": touch_ends(jax.random.randint(streams_of[1], (ORBITALS, 3), 0, BOX // 2), jax.random.fold_in(streams_of[1], 1), 0, (BOX // 2) - 1).astype(jnp.int32),
        "pick": touch_ends(jax.random.randint(streams_of[2], (N_GRP, N_DEV, N_GRP), 0, ORB_DEV), jax.random.fold_in(streams_of[2], 1), 0, ORB_DEV - 1).astype(jnp.int32),
        "pair_local": touch_ends(jax.random.randint(streams_of[3], (N_GRP, N_DEV, PAIRS), 0, ORB_DEV), jax.random.fold_in(streams_of[3], 1), 0, ORB_DEV - 1).astype(jnp.int32),
        "pair_source": draw_pair_source(jax.random.fold_in(streams_of[6], 71), 0),
        "pair_count": draw_pair_count(jax.random.fold_in(streams_of[6], 71), 0),
    }


def tables(box_side):
    freq = jnp.arange(box_side, dtype=jnp.int32)
    angle_step = math.pi / (box_side + 1)
    phase = (freq[:, None] + 1) * (freq[None, :] + 1) % (2 * (box_side + 1))
    sine_table = math.sqrt(2.0 / (box_side + 1)) * jnp.sin(angle_step * phase.astype(jnp.float32))
    modes = 2.0 - 2.0 * jnp.cos(angle_step * (freq.astype(jnp.float32) + 1.0))
    eigen_sum = modes[:, None, None] + modes[None, :, None] + modes[None, None, :]
    return (sine_table, eigen_sum.reshape(box_side, box_side * box_side))

def turn(matrix, a_field, box_side):
    product = jnp.dot(matrix, a_field, preferred_element_type=jnp.float32, precision=lax.Precision.HIGHEST)
    return product.reshape(box_side, box_side, box_side).transpose(1, 2, 0).reshape(box_side, box_side * box_side)

def pair_terms(phi_i, phi_j, offset_gap, sine_table, eigen_sum):
    box_side = phi_i.shape[0]
    box_rows = jnp.arange(box_side, dtype=jnp.int32)
    shifters = [box_rows[:, None] + offset_gap[which_axis] == box_rows[None, :] for which_axis in range(3)]
    moved = phi_j
    for shifter in shifters:
        moved = turn(shifter.astype(jnp.bfloat16), moved, box_side).astype(jnp.bfloat16)
    moved_wide = moved.astype(jnp.float32)
    own_wide = phi_i.astype(jnp.float32)
    spectrum = own_wide * moved_wide
    for repeat in range(3):
        spectrum = turn(sine_table, spectrum, box_side)
    spectrum = spectrum / eigen_sum
    for repeat in range(3):
        spectrum = turn(sine_table, spectrum, box_side)
    own_term = spectrum * moved_wide
    backward = spectrum * own_wide
    for shifter in shifters:
        backward = turn(shifter.T.astype(jnp.float32), backward, box_side)
    return (own_term, backward)

def reference(orbitals, offsets, pick, pair_local, pair_source, pair_count):
    sine_table, eigen_sum = tables(BOX)
    box_cells = BOX * BOX * BOX
    slot_range = jnp.arange(N_GRP, dtype=jnp.int32)

    def device_step(total, flat_dev):
        grp_index = flat_dev // N_DEV
        dev_index = flat_dev % N_DEV
        own_slots = pair_local[grp_index, dev_index]
        src_slots = pair_source[grp_index, dev_index]
        listed = pair_count[grp_index, dev_index, 0]
        partner_ids = ((slot_range * N_DEV + dev_index) * ORB_DEV + pick[:, dev_index, grp_index]).astype(jnp.int32)
        first_orb = (flat_dev * ORB_DEV).astype(jnp.int32)
        own_boxes = lax.dynamic_slice_in_dim(orbitals, first_orb, ORB_DEV, 0)
        own_offs = lax.dynamic_slice_in_dim(offsets, first_orb, ORB_DEV, 0)

        def pair_step(state_pair, pair_index):

            def work(inner):
                own_sum, returned = inner
                own_slot = own_slots[pair_index]
                src_slot = src_slots[pair_index]
                partner = partner_ids[src_slot]
                offset_gap = own_offs[own_slot] - offsets[partner]
                own_term, backward = pair_terms(own_boxes[own_slot], orbitals[partner], offset_gap, sine_table, eigen_sum)
                return (own_sum.at[own_slot].add(own_term), returned.at[src_slot].add(backward))

            def keep(inner):
                return inner
            return (lax.cond(pair_index < listed, work, keep, state_pair), None)
        start = (jnp.zeros((ORB_DEV, BOX, BOX * BOX), jnp.float32), jnp.zeros((N_GRP, BOX, BOX * BOX), jnp.float32))
        (own_sum, returned), unused = lax.scan(pair_step, start, jnp.arange(PAIRS, dtype=jnp.int32))
        current = lax.dynamic_slice_in_dim(total, first_orb, ORB_DEV, 0)
        total = lax.dynamic_update_slice_in_dim(total, current + own_sum.reshape(ORB_DEV, box_cells), first_orb, 0)
        rounded = lax.optimization_barrier(returned.astype(jnp.bfloat16)).astype(jnp.float32)
        total = total.at[partner_ids].add(rounded.reshape(N_GRP, box_cells))
        return (total, None)
    total = jnp.zeros((ORBITALS, box_cells), jnp.float32)
    total, unused = lax.scan(device_step, total, jnp.arange(N_GRP * N_DEV, dtype=jnp.int32))
    return total
```

```python
import functools
import math

import numpy as np

import jax
import jax.numpy as jnp
from jax import lax
from jax.experimental import pallas as pl
from jax.experimental.pallas import tpu as pltpu
from jax.sharding import PartitionSpec as P

LANES = 128
HALF = 64
f32 = jnp.float32
bf16 = jnp.bfloat16


def np_tables(n):
    freq = np.arange(n)
    step = math.pi / (n + 1)
    sine = math.sqrt(2.0 / (n + 1)) * np.sin(step * ((freq[:, None] + 1) * (freq[None, :] + 1) % (2 * (n + 1))))
    sine = sine.astype(np.float32)
    high = sine.astype(jnp.bfloat16)
    low = (sine - high.astype(np.float32)).astype(jnp.bfloat16)

    def two(block):
        out = np.zeros((LANES, LANES), jnp.bfloat16)
        out[:n, :n] = block
        out[HALF : HALF + n, HALF : HALF + n] = block
        return out

    lane_side = np.block([[two(high), two(low)], [two(high), two(low)]])
    row_side = np.concatenate([high, high, low, low], axis=1)
    modes = (2.0 - 2.0 * np.cos(step * (freq + 1.0))).astype(np.float32)
    base = np.ones((n, LANES), np.float32)
    outer = np.ones((n // 2, LANES), np.float32)
    for half in range(2):
        at = half * HALF
        base[:, at : at + n] = modes[:, None] + modes[None, :]
        outer[:, at : at + HALF] = modes[half * (n // 2) : (half + 1) * (n // 2), None]
    return lane_side, row_side, base, outer


def split(x):
    high = x.astype(bf16)
    return high, (x - high.astype(f32)).astype(bf16)


def lane_turn(x, lane_side):
    both = jnp.concatenate(split(x), axis=1)
    out = jnp.dot(both, lane_side, preferred_element_type=f32)
    return out[:, :LANES] + out[:, LANES:]


def row_turn(tiles, row_side):
    columns = []
    for tile in tiles:
        high, low = split(tile)
        columns.append(jnp.concatenate([high, low, high, low], axis=0))
    out = jnp.dot(row_side, jnp.concatenate(columns, axis=1), preferred_element_type=f32)
    return out[:, :LANES], out[:, LANES:]


def pair_kernel(sizes, step, first, last, *refs):
    n, orbs, slots, groups = sizes
    half = n // 2
    cells_tile = half * n // LANES
    wide = n + 2 * half
    chunk = 6 if half % 6 == 0 else 2
    meta, where_am_i, own = refs[:3]
    others = refs[3 : 3 + orbs]
    lane_ref, row_ref, base_ref, outer_ref = refs[3 + orbs : 7 + orbs]
    rest = list(refs[7 + orbs :])
    total_in = None if first else rest.pop(0)
    total_out = None if last else rest.pop(0)
    out = rest.pop(0) if last else None
    total = rest.pop(0) if last else total_out
    dense_i, dense_j, held_i, held_j, moved, field, other = rest

    lane = lax.broadcasted_iota(jnp.int32, (n, LANES), 1)
    row = lax.broadcasted_iota(jnp.int32, (n, LANES), 0)
    left = lane < HALF
    left_half = left[:half]
    if first:
        total[...] = jnp.zeros_like(total)
    else:
        total[...] = total_in[...]

    at_source = 3 * orbs + slots
    at_count = at_source + slots
    at_pick = at_count + 1
    me = where_am_i[0]
    them = lax.rem(me + groups - step, groups)

    def unpack(dense, put):
        for yo in range(half):
            start = yo * n % LANES
            first_tile = yo * n // LANES
            halves = []
            for h in range(2):
                t = (first_tile + h * cells_tile) * LANES
                piece = dense[:, t : t + LANES].astype(f32)
                if start + n > LANES:
                    after = dense[:, t + LANES : t + 2 * LANES].astype(f32)
                    piece = jnp.where(lane >= start, piece, after)
                amount = (h * HALF - start) % LANES
                halves.append(pltpu.roll(piece, amount, 1) if amount else piece)
            put(yo, jnp.where(left, halves[0], halves[1]))

    def shifted(gap, use):
        gap_x, gap_y, gap_z = gap
        z_at = lax.rem(lane, HALF)
        inside = (
            (z_at < n)
            & (z_at + gap_z >= 0)
            & (z_at + gap_z < n)
            & (row + gap_x >= 0)
            & (row + gap_x < n)
        )
        for yo in range(half):
            s = gap_y + yo
            under = s < 0
            over = s >= half
            src = s + jnp.where(under, half, 0) - jnp.where(over, half, 0)
            tile = held_j[pl.ds(src * wide + half + gap_x, n), :]
            amount = (2 * LANES - gap_z + jnp.where(under | over, HALF, 0)) % LANES
            tile = pltpu.roll(tile, amount, 1)
            low_lane = jnp.where(under, HALF, 0)
            high_lane = jnp.where(over, HALF, LANES)
            good = inside & (lane >= low_lane) & (lane < high_lane)
            use(yo, jnp.where(good, tile, 0.0))

    def swapped(ref, at):
        a = ref[pl.ds(at, half, stride=n), :]
        b = ref[pl.ds(at + half, half, stride=n), :]
        top = jnp.where(left_half, a, pltpu.roll(b, HALF, 1))
        bottom = jnp.where(left_half, pltpu.roll(a, HALF, 1), b)
        return jnp.concatenate([top, bottom], axis=0)

    def task(which, carry):
        lister = jnp.where(which == 0, me, them)
        source = jnp.where(which == 0, them, me)
        listed = meta[lister, at_count]
        i_at = jnp.int32(0)
        found = jnp.int32(0)
        for p in range(slots):
            hit = (meta[lister, at_source + p] == source) & (p < listed)
            i_at = jnp.where(hit, meta[lister, 3 * orbs + p], i_at)
            found = jnp.where(hit, 1, found)
        j_at = meta[source, at_pick + lister]
        gap = [meta[lister, i_at * 3 + k] - meta[source, j_at * 3 + k] for k in range(3)]

        @pl.when(found == 1)
        def _():
            @pl.when(which == 0)
            def _():
                dense_i[...] = own[i_at]
                for q in range(orbs):
                    @pl.when(j_at == q)
                    def _():
                        dense_j[...] = others[q][...]

            @pl.when(which == 1)
            def _():
                dense_j[...] = own[j_at]
                for q in range(orbs):
                    @pl.when(i_at == q)
                    def _():
                        dense_i[...] = others[q][...]

            def put_i(yo, tile):
                held_i[yo * n : (yo + 1) * n, :] = tile

            def put_j(yo, tile):
                held_j[yo * wide + half : yo * wide + half + n, :] = tile

            unpack(dense_i, put_i)
            unpack(dense_j, put_j)

            def use_moved(yo, tile):
                moved[yo * n : (yo + 1) * n, :] = tile

            shifted(gap, use_moved)
            lane_side = lane_ref[...]
            row_side = row_ref[...]
            rows = chunk * n
            for c in range(half // chunk):
                here = slice(c * rows, (c + 1) * rows)
                spectrum = lane_turn(held_i[here, :] * moved[here, :], lane_side)
                for q in range(0, chunk, 2):
                    pair = row_turn([spectrum[(q + k) * n : (q + k + 1) * n] for k in range(2)], row_side)
                    for k in range(2):
                        at = c * rows + (q + k) * n
                        field[at : at + n, :] = pair[k]
            for xo in range(0, half, 2):
                pair = row_turn([swapped(field, xo + k) for k in range(2)], row_side)
                pair = [pair[k] / (base_ref[...] + outer_ref[xo + k : xo + k + 1, :]) for k in range(2)]
                pair = row_turn(pair, row_side)
                for k in range(2):
                    other[(xo + k) * n : (xo + k + 1) * n, :] = pair[k]
            for c in range(half // chunk):
                tiles = []
                for q in range(0, chunk, 2):
                    tiles += row_turn([swapped(other, c * chunk + q + k) for k in range(2)], row_side)
                field[c * rows : (c + 1) * rows, :] = lane_turn(jnp.concatenate(tiles, axis=0), lane_side)

            @pl.when(which == 0)
            def _():
                for yo in range(half):
                    here = slice(yo * n, (yo + 1) * n)
                    there = pl.ds(i_at * (half * n) + yo * n, n)
                    total[there, :] += field[here, :] * moved[here, :]

            @pl.when(which == 1)
            def _():
                for yo in range(half):
                    here = slice(yo * n, (yo + 1) * n)
                    put_j(yo, (field[here, :] * held_i[here, :]).astype(bf16).astype(f32))

                def add_back(yo, tile):
                    there = pl.ds(j_at * (half * n) + yo * n, n)
                    total[there, :] += tile

                shifted([-k for k in gap], add_back)

        return carry

    lax.fori_loop(0, 2, task, 0)

    if last:
        for a in range(orbs):
            current = {}
            for yo in range(half):
                start = yo * n % LANES
                first_tile = yo * n // LANES
                tile = total[a * half * n + yo * n : a * half * n + (yo + 1) * n, :]
                for h in range(2):
                    t = first_tile + h * cells_tile
                    amount = (start - h * HALF) % LANES
                    piece = pltpu.roll(tile, amount, 1) if amount else tile
                    current[t] = jnp.where(lane >= start, piece, current[t]) if t in current else piece
                    if start + n >= LANES:
                        out[a, :, t * LANES : (t + 1) * LANES] = current.pop(t).astype(bf16)
                        if start + n > LANES:
                            current[t + 1] = piece


def pair_step(step, first, last, meta, where_am_i, own, others, tables, total):
    orbs, n, plane = own.shape
    groups = meta.shape[0]
    half = n // 2
    slots = (meta.shape[1] - 3 * orbs - 1 - groups) // 2
    vmem = pl.BlockSpec(memory_space=pltpu.VMEM)
    smem = pl.BlockSpec(memory_space=pltpu.SMEM)
    operands = [meta, where_am_i, own, *others, *tables]
    specs = [smem, smem] + [vmem] * (1 + orbs + len(tables))
    if not first:
        operands.append(total)
        specs.append(vmem)
    held = jax.ShapeDtypeStruct((orbs * half * n, LANES), f32)
    rows = half * n
    scratch = [
        pltpu.VMEM((n, plane), bf16),
        pltpu.VMEM((n, plane), bf16),
        pltpu.VMEM((rows, LANES), f32),
        pltpu.VMEM((half * (n + 2 * half), LANES), f32),
        pltpu.VMEM((rows, LANES), f32),
        pltpu.VMEM((rows, LANES), f32),
        pltpu.VMEM((rows, LANES), f32),
    ]
    if last:
        scratch.insert(0, pltpu.VMEM(held.shape, f32))
    return pl.pallas_call(
        functools.partial(pair_kernel, (n, orbs, slots, groups), step, first, last),
        out_shape=jax.ShapeDtypeStruct(own.shape, bf16) if last else held,
        in_specs=specs,
        out_specs=vmem,
        scratch_shapes=scratch,
        compiler_params=pltpu.CompilerParams(vmem_limit_bytes=32 << 20),
        cost_estimate=pl.CostEstimate(flops=2 * 12 * 3 * n**4, bytes_accessed=4 * n**3 * 4, transcendentals=0),
        name=f"pairs_{step}",
    )(*operands)


def body(orbitals, offsets, pick, pair_local, pair_source, pair_count):
    orbs, n, plane = orbitals.shape
    groups = lax.axis_size("grp")
    me = lax.axis_index("grp").astype(jnp.int32)
    member = lax.axis_index("dev")
    my_pick = lax.dynamic_slice_in_dim(pick[0], member, 1, 0)[0]
    mine = jnp.concatenate(
        [offsets.reshape(-1), pair_local[0, 0], pair_source[0, 0], pair_count[0, 0], my_pick]
    ).astype(jnp.int32)
    ring = [(g, (g + 1) % groups) for g in range(groups)]
    held = [orbitals[q] for q in range(orbs)]
    tables = [jnp.asarray(t) for t in np_tables(n)]
    meta = None
    total = None
    for step in range(1, groups):
        held = [lax.ppermute(h, "grp", ring) for h in held]
        if meta is None:
            meta = lax.all_to_all(
                jnp.broadcast_to(mine[None, :], (groups, mine.shape[0])), "grp", 0, 0, tiled=True
            )
        total = pair_step(
            step, step == 1, step == groups - 1, meta, me.reshape(1), orbitals, held, tables, total
        )
    whole = total.reshape(orbs, n * plane)
    return lax.all_to_all(whole, "dev", split_axis=1, concat_axis=0, tiled=True).astype(f32)


def solution(mesh):
    return jax.shard_map(
        body,
        mesh=mesh,
        in_specs=(
            P(("grp", "dev"), None, None),
            P(("grp", "dev"), None),
            P("grp", None, None),
            P("grp", "dev", None),
            P("grp", "dev", None),
            P("grp", "dev", None),
        ),
        out_specs=P("grp", "dev"),
        check_vma=False,
    )
```

```python
import functools
import math

import numpy as np

import jax
import jax.numpy as jnp
from jax import lax
from jax.experimental import pallas as pl
from jax.experimental.pallas import tpu as pltpu
from jax.sharding import PartitionSpec as P

LANES = 128
HALF = 64
f32 = jnp.float32
bf16 = jnp.bfloat16


def np_tables(n):
    freq = np.arange(n)
    step = math.pi / (n + 1)
    sine = math.sqrt(2.0 / (n + 1)) * np.sin(step * ((freq[:, None] + 1) * (freq[None, :] + 1) % (2 * (n + 1))))
    sine = sine.astype(np.float32)
    high = sine.astype(jnp.bfloat16)
    low = (sine - high.astype(np.float32)).astype(jnp.bfloat16)

    def two(block):
        out = np.zeros((LANES, LANES), jnp.bfloat16)
        out[:n, :n] = block
        out[HALF : HALF + n, HALF : HALF + n] = block
        return out

    lane_side = np.block([[two(high), two(low)], [two(high), two(low)]])
    row_side = np.concatenate([high, high, low, low], axis=1)
    modes = (2.0 - 2.0 * np.cos(step * (freq + 1.0))).astype(np.float32)
    base = np.ones((n, LANES), np.float32)
    outer = np.ones((n // 2, LANES), np.float32)
    for half in range(2):
        at = half * HALF
        base[:, at : at + n] = modes[:, None] + modes[None, :]
        outer[:, at : at + HALF] = modes[half * (n // 2) : (half + 1) * (n // 2), None]
    pad = np.zeros((n, 2 * LANES - 4 * n), jnp.bfloat16)
    return np.concatenate([lane_side, np.concatenate([row_side, pad], axis=1)]), np.concatenate([base, outer])


def split(x):
    high = x.astype(bf16)
    return high, (x - high.astype(f32)).astype(bf16)


def lane_turn(x, lane_side):
    both = jnp.concatenate(split(x), axis=1)
    out = jnp.dot(both, lane_side, preferred_element_type=f32)
    return out[:, :LANES] + out[:, LANES:]


def row_turn(tiles, row_side):
    columns = []
    for tile in tiles:
        high, low = split(tile)
        columns.append(jnp.concatenate([high, low, high, low], axis=0))
    out = jnp.dot(row_side, jnp.concatenate(columns, axis=1), preferred_element_type=f32)
    return out[:, :LANES], out[:, LANES:]


def pair_kernel(sizes, pieces, first, last, *refs):
    n, orbs, slots = sizes
    half = n // 2
    cells_tile = half * n // LANES
    wide = n + 2 * half
    chunk = 6 if half % 6 == 0 else 2
    mine, theirs, own = refs[:3]
    others = refs[3 : 3 + orbs]
    sines, modes = refs[3 + orbs : 5 + orbs]
    rest = list(refs[5 + orbs :])
    total_in = None if first else rest.pop(0)
    if last:
        outs = [rest.pop(0) for _ in range(max(pieces, 1))]
        total = rest.pop(0)
        flat = rest.pop(0) if pieces else None
    else:
        total = rest.pop(0)
    dense_i, dense_j, held_i, held_j, moved, field, other = rest

    lane = lax.broadcasted_iota(jnp.int32, (n, LANES), 1)
    row = lax.broadcasted_iota(jnp.int32, (n, LANES), 0)
    left = lane < HALF
    left_half = left[:half]
    if first:
        total[...] = jnp.zeros_like(total)
    else:
        total[...] = total_in[...]

    at_source = 3 * orbs + slots
    at_count = at_source + slots
    at_group = at_count + 1
    at_pick = at_group + 2
    me = mine[0, at_group]
    them = theirs[0, at_group]
    member = mine[0, at_group + 1]

    def unpack(dense, put):
        for yo in range(half):
            start = yo * n % LANES
            first_tile = yo * n // LANES
            halves = []
            for h in range(2):
                t = (first_tile + h * cells_tile) * LANES
                piece = dense[:, t : t + LANES].astype(f32)
                if start + n > LANES:
                    after = dense[:, t + LANES : t + 2 * LANES].astype(f32)
                    piece = jnp.where(lane >= start, piece, after)
                amount = (h * HALF - start) % LANES
                halves.append(pltpu.roll(piece, amount, 1) if amount else piece)
            put(yo, jnp.where(left, halves[0], halves[1]))

    def shifted(gap, use):
        gap_x, gap_y, gap_z = gap
        z_at = lax.rem(lane, HALF)
        inside = (
            (z_at < n)
            & (z_at + gap_z >= 0)
            & (z_at + gap_z < n)
            & (row + gap_x >= 0)
            & (row + gap_x < n)
        )
        for yo in range(half):
            s = gap_y + yo
            under = s < 0
            over = s >= half
            src = s + jnp.where(under, half, 0) - jnp.where(over, half, 0)
            tile = held_j[pl.ds(src * wide + half + gap_x, n), :]
            amount = (2 * LANES - gap_z + jnp.where(under | over, HALF, 0)) % LANES
            tile = pltpu.roll(tile, amount, 1)
            low_lane = jnp.where(under, HALF, 0)
            high_lane = jnp.where(over, HALF, LANES)
            good = inside & (lane >= low_lane) & (lane < high_lane)
            use(yo, jnp.where(good, tile, 0.0))

    def swapped(ref, at):
        a = ref[pl.ds(at, half, stride=n), :]
        b = ref[pl.ds(at + half, half, stride=n), :]
        top = jnp.where(left_half, a, pltpu.roll(b, HALF, 1))
        bottom = jnp.where(left_half, pltpu.roll(a, HALF, 1), b)
        return jnp.concatenate([top, bottom], axis=0)

    def task(which, carry):
        outgoing = which == 0

        def lister(k):
            return jnp.where(outgoing, mine[0, k], theirs[0, k])

        def source(k):
            return jnp.where(outgoing, theirs[0, k], mine[0, k])

        lister_group = jnp.where(outgoing, me, them)
        source_group = jnp.where(outgoing, them, me)
        listed = lister(at_count)
        i_at = jnp.int32(0)
        found = jnp.int32(0)
        for p in range(slots):
            hit = (lister(at_source + p) == source_group) & (p < listed)
            i_at = jnp.where(hit, lister(3 * orbs + p), i_at)
            found = jnp.where(hit, 1, found)
        j_at = source(at_pick + lister_group)
        gap = [lister(i_at * 3 + k) - source(j_at * 3 + k) for k in range(3)]

        @pl.when(found == 1)
        def _():
            @pl.when(which == 0)
            def _():
                dense_i[...] = own[i_at]
                for q in range(orbs):
                    @pl.when(j_at == q)
                    def _():
                        dense_j[...] = others[q][...]

            @pl.when(which == 1)
            def _():
                dense_j[...] = own[j_at]
                for q in range(orbs):
                    @pl.when(i_at == q)
                    def _():
                        dense_i[...] = others[q][...]

            def put_i(yo, tile):
                held_i[yo * n : (yo + 1) * n, :] = tile

            def put_j(yo, tile):
                held_j[yo * wide + half : yo * wide + half + n, :] = tile

            unpack(dense_i, put_i)
            unpack(dense_j, put_j)

            def use_moved(yo, tile):
                moved[yo * n : (yo + 1) * n, :] = tile

            shifted(gap, use_moved)
            lane_side = sines[: 2 * LANES, :]
            row_side = sines[2 * LANES :, : 4 * n]
            rows = chunk * n
            for c in range(half // chunk):
                here = slice(c * rows, (c + 1) * rows)
                spectrum = lane_turn(held_i[here, :] * moved[here, :], lane_side)
                for q in range(0, chunk, 2):
                    pair = row_turn([spectrum[(q + k) * n : (q + k + 1) * n] for k in range(2)], row_side)
                    for k in range(2):
                        at = c * rows + (q + k) * n
                        field[at : at + n, :] = pair[k]
            for xo in range(0, half, 2):
                pair = row_turn([swapped(field, xo + k) for k in range(2)], row_side)
                pair = [pair[k] / (modes[:n, :] + modes[n + xo + k : n + xo + k + 1, :]) for k in range(2)]
                pair = row_turn(pair, row_side)
                for k in range(2):
                    other[(xo + k) * n : (xo + k + 1) * n, :] = pair[k]
            for c in range(half // chunk):
                tiles = []
                for q in range(0, chunk, 2):
                    tiles += row_turn([swapped(other, c * chunk + q + k) for k in range(2)], row_side)
                field[c * rows : (c + 1) * rows, :] = lane_turn(jnp.concatenate(tiles, axis=0), lane_side)

            @pl.when(which == 0)
            def _():
                for yo in range(half):
                    here = slice(yo * n, (yo + 1) * n)
                    there = pl.ds(i_at * (half * n) + yo * n, n)
                    total[there, :] += field[here, :] * moved[here, :]

            @pl.when(which == 1)
            def _():
                for yo in range(half):
                    here = slice(yo * n, (yo + 1) * n)
                    put_j(yo, (field[here, :] * held_i[here, :]).astype(bf16).astype(f32))

                def add_back(yo, tile):
                    there = pl.ds(j_at * (half * n) + yo * n, n)
                    total[there, :] += tile

                shifted([-k for k in gap], add_back)

        return carry

    lax.fori_loop(0, 2, task, 0)

    if last:
        for a in range(orbs):
            current = {}
            for yo in range(half):
                start = yo * n % LANES
                first_tile = yo * n // LANES
                tile = total[a * half * n + yo * n : a * half * n + (yo + 1) * n, :]
                for h in range(2):
                    t = first_tile + h * cells_tile
                    amount = (start - h * HALF) % LANES
                    piece = pltpu.roll(tile, amount, 1) if amount else tile
                    current[t] = jnp.where(lane >= start, piece, current[t]) if t in current else piece
                    if start + n >= LANES:
                        here = slice(t * LANES, (t + 1) * LANES)
                        if pieces:
                            flat[pl.ds(t * orbs * n + a, n, stride=orbs), :] = current.pop(t)
                        else:
                            outs[0][a, :, here] = current.pop(t).astype(bf16)
                        if start + n > LANES:
                            current[t + 1] = piece
        depth = n // pieces * orbs if pieces else 0
        tiles = n * n // LANES
        for k in range(pieces):
            at = jnp.bitwise_xor(member, k) * depth
            for t in range(tiles):
                outs[k][:, t * LANES : (t + 1) * LANES] = flat[pl.ds(t * orbs * n + at, 8), :].astype(bf16)
            for t in range(tiles // 2):
                tail = [flat[pl.ds((t + h * tiles // 2) * orbs * n + at + 8, 4), :] for h in range(2)]
                tail_at = (tiles + t) * LANES
                outs[k][:, tail_at : tail_at + LANES] = jnp.concatenate(tail, axis=0).astype(bf16)


def pair_step(step, pieces, first, last, mine, theirs, own, others, tables, total):
    orbs, n, plane = own.shape
    half = n // 2
    slots = pieces[1]
    pieces = pieces[0] if last else 0
    vmem = pl.BlockSpec(memory_space=pltpu.VMEM)
    smem = pl.BlockSpec(memory_space=pltpu.SMEM)
    operands = [mine, theirs, own, *others, *tables]
    specs = [smem, smem] + [vmem] * (1 + orbs + len(tables))
    if not first:
        operands.append(total)
        specs.append(vmem)
    held = jax.ShapeDtypeStruct((orbs * half * n, LANES), f32)
    rows = half * n
    scratch = [
        pltpu.VMEM((n, plane), bf16),
        pltpu.VMEM((n, plane), bf16),
        pltpu.VMEM((rows, LANES), f32),
        pltpu.VMEM((half * (n + 2 * half), LANES), f32),
        pltpu.VMEM((rows, LANES), f32),
        pltpu.VMEM((rows, LANES), f32),
        pltpu.VMEM((rows, LANES), f32),
    ]
    shapes = held
    if last:
        shapes = jax.ShapeDtypeStruct(own.shape, bf16)
        if pieces:
            scratch.insert(0, pltpu.VMEM((orbs * n * plane // LANES, LANES), f32))
            shapes = [jax.ShapeDtypeStruct((8, orbs * n * plane // pieces // 8), bf16)] * pieces
        scratch.insert(0, pltpu.VMEM(held.shape, f32))
    return pl.pallas_call(
        functools.partial(pair_kernel, (n, orbs, slots), pieces, first, last),
        out_shape=shapes,
        in_specs=specs,
        out_specs=[vmem] * pieces if pieces else vmem,
        scratch_shapes=scratch,
        compiler_params=pltpu.CompilerParams(vmem_limit_bytes=32 << 20),
        cost_estimate=pl.CostEstimate(flops=2 * 12 * 3 * n**4, bytes_accessed=4 * n**3 * 4, transcendentals=0),
        name=f"pairs_{step}",
    )(*operands)


def gather_kernel(n, orbs, member_ref, *refs):
    devices = len(refs) - 3
    out, rows, mixed = refs[devices:]
    tiles = n * n // LANES
    member = member_ref[0]
    for k in range(devices):
        at = pl.multiple_of(jnp.bitwise_xor(member, k) * 8, 8)
        for t in range(tiles * 3 // 2):
            rows[pl.ds(t * devices * 8 + at, 8), :] = refs[k][:, t * LANES : (t + 1) * LANES].astype(f32)
    for x in range(n // devices):
        for t in range(tiles):
            here = slice((x * tiles + t) * LANES, (x * tiles + t + 1) * LANES)
            at = (x * tiles + t) * orbs * devices
            for a in range(orbs):
                q = x * orbs + a
                tile = t
                if q >= 8:
                    q += 4 * (t * 2 // tiles) - 8
                    tile = tiles + t % (tiles // 2)
                mixed[pl.ds(at + a, devices, stride=orbs), :] = rows[
                    pl.ds(tile * devices * 8 + q, devices, stride=8), :
                ]
            out[:, here] = mixed[at : at + orbs * devices, :]


def body(orbitals, offsets, pick, pair_local, pair_source, pair_count):
    orbs, n, plane = orbitals.shape
    groups = lax.axis_size("grp")
    devices = lax.axis_size("dev")
    me = lax.axis_index("grp").astype(jnp.int32)
    member = lax.axis_index("dev").astype(jnp.int32)
    my_pick = lax.dynamic_slice_in_dim(pick[0], member, 1, 0)[0]
    mine = jnp.concatenate(
        [
            offsets.reshape(-1),
            pair_local[0, 0],
            pair_source[0, 0],
            pair_count[0, 0],
            me.reshape(1),
            member.reshape(1),
            my_pick,
        ]
    ).astype(jnp.int32)[None, :]
    by_pieces = devices & (devices - 1) == 0 and n % devices == 0 and n // devices * orbs == 12
    pieces = devices if by_pieces else 0
    ring = [(g, (g + 1) % groups) for g in range(groups)]
    held = [orbitals[q] for q in range(orbs)]
    tables = [jnp.asarray(t) for t in np_tables(n)]
    theirs = mine
    total = None
    for step in range(1, groups):
        held = [lax.ppermute(h, "grp", ring) for h in held]
        theirs = lax.ppermute(theirs, "grp", ring)
        held[0], theirs, total = lax.optimization_barrier((held[0], theirs, total))
        total = pair_step(
            step,
            (pieces, pair_local.shape[2]),
            step == 1,
            step == groups - 1,
            mine,
            theirs,
            orbitals,
            held,
            tables,
            total,
        )
    if not pieces:
        whole = total.reshape(orbs, n * plane)
        return lax.all_to_all(whole, "dev", split_axis=1, concat_axis=0, tiled=True).astype(f32)
    arrived = [total[0]]
    for k in range(1, devices):
        arrived.append(lax.ppermute(total[k], "dev", [(d, d ^ k) for d in range(devices)]))
    vmem = pl.BlockSpec(memory_space=pltpu.VMEM)
    return pl.pallas_call(
        functools.partial(gather_kernel, n, orbs),
        out_shape=jax.ShapeDtypeStruct((orbs * devices, n * plane // devices), f32),
        in_specs=[pl.BlockSpec(memory_space=pltpu.SMEM)] + [vmem] * devices,
        out_specs=vmem,
        scratch_shapes=[pltpu.VMEM((orbs * n * plane // LANES, LANES), f32)] * 2,
        compiler_params=pltpu.CompilerParams(vmem_limit_bytes=32 << 20),
        name="cells",
    )(member.reshape(1), *arrived)


def solution(mesh):
    return jax.shard_map(
        body,
        mesh=mesh,
        in_specs=(
            P(("grp", "dev"), None, None),
            P(("grp", "dev"), None),
            P("grp", None, None),
            P("grp", "dev", None),
            P("grp", "dev", None),
            P("grp", "dev", None),
        ),
        out_specs=P("grp", "dev"),
        check_vma=False,
    )
```

```python
import functools
import math

import numpy as np

import jax
import jax.numpy as jnp
from jax import lax
from jax.experimental import pallas as pl
from jax.experimental.pallas import tpu as pltpu
from jax.sharding import PartitionSpec as P

LANES = 128
HALF = 64
ROWS = 16
f32 = jnp.float32
bf16 = jnp.bfloat16


def np_tables(n):
    freq = np.arange(n)
    step = math.pi / (n + 1)
    sine = math.sqrt(2.0 / (n + 1)) * np.sin(step * ((freq[:, None] + 1) * (freq[None, :] + 1) % (2 * (n + 1))))
    sine = sine.astype(np.float32)
    high = sine.astype(jnp.bfloat16)
    low = (sine - high.astype(np.float32)).astype(jnp.bfloat16)

    def two(block):
        out = np.zeros((LANES, LANES), jnp.bfloat16)
        out[:n, :n] = block
        out[HALF : HALF + n, HALF : HALF + n] = block
        return out

    lane_side = np.block([[two(high), two(low)], [two(high), two(low)]])
    row_side = np.concatenate([high, high, low, low], axis=1)
    modes = (2.0 - 2.0 * np.cos(step * (freq + 1.0))).astype(np.float32)
    base = np.ones((n, LANES), np.float32)
    outer = np.ones((n // 2, LANES), np.float32)
    for half in range(2):
        at = half * HALF
        base[:, at : at + n] = modes[:, None] + modes[None, :]
        outer[:, at : at + HALF] = modes[half * (n // 2) : (half + 1) * (n // 2), None]
    pad = np.zeros((n, 2 * LANES - 4 * n), jnp.bfloat16)
    sines = np.concatenate([lane_side, np.concatenate([row_side, pad], axis=1)]).astype(np.float32)
    modes = np.concatenate([base, outer])
    modes = np.pad(modes, ((0, len(sines) - len(modes)), (0, 0)))
    return np.concatenate([sines, modes], axis=1)


def split(x):
    high = x.astype(bf16)
    return high, (x - high.astype(f32)).astype(bf16)


def lane_turn(x, lane_side):
    both = jnp.concatenate(split(x), axis=1)
    out = jnp.dot(both, lane_side, preferred_element_type=f32)
    return out[:, :LANES] + out[:, LANES:]


def row_turn(tiles, row_side):
    columns = []
    for tile in tiles:
        high, low = split(tile)
        columns.append(jnp.concatenate([high, low, high, low], axis=0))
    out = jnp.dot(row_side, jnp.concatenate(columns, axis=1), preferred_element_type=f32)
    return out[:, :LANES], out[:, LANES:]


def pair_kernel(sizes, pieces, first, last, *refs):
    n, orbs, slots = sizes
    half = n // 2
    cells_tile = half * n // LANES
    wide = n + 2 * half
    chunk = 6 if half % 6 == 0 else 2
    mine, own = refs[:2]
    others = refs[2 : 2 + orbs]
    table = refs[2 + orbs]
    rest = list(refs[3 + orbs :])
    total_in = None if first else rest.pop(0)
    if last:
        outs = [rest.pop(0) for _ in range(max(pieces, 1))]
        total = rest.pop(0)
        flat = rest.pop(0) if pieces else None
    else:
        total = rest.pop(0)
    dense_i, dense_j, held_i, held_j, moved, field, other, theirs = rest
    lists = others[-1][:, n * n * n // ROWS :].astype(f32).astype(jnp.int32)
    for k in range(mine.shape[1]):
        theirs[0, k] = lists[0, k]

    def fetch(dense, q):
        if q < orbs - 1:
            dense[...] = others[q][...]
        else:
            for r in range(n // ROWS):
                dense[r * ROWS : (r + 1) * ROWS, :] = others[q][:, r * n * n : (r + 1) * n * n]

    lane = lax.broadcasted_iota(jnp.int32, (n, LANES), 1)
    row = lax.broadcasted_iota(jnp.int32, (n, LANES), 0)
    left = lane < HALF
    left_half = left[:half]
    if first:
        total[...] = jnp.zeros_like(total)
    else:
        total[...] = total_in[...]

    at_source = 3 * orbs + slots
    at_count = at_source + slots
    at_group = at_count + 1
    at_pick = at_group + 2
    me = mine[0, at_group]
    them = theirs[0, at_group]
    member = mine[0, at_group + 1]

    def unpack(dense, put):
        for yo in range(half):
            start = yo * n % LANES
            first_tile = yo * n // LANES
            halves = []
            for h in range(2):
                t = (first_tile + h * cells_tile) * LANES
                piece = dense[:, t : t + LANES].astype(f32)
                if start + n > LANES:
                    after = dense[:, t + LANES : t + 2 * LANES].astype(f32)
                    piece = jnp.where(lane >= start, piece, after)
                amount = (h * HALF - start) % LANES
                halves.append(pltpu.roll(piece, amount, 1) if amount else piece)
            put(yo, jnp.where(left, halves[0], halves[1]))

    def shifted(gap, use):
        gap_x, gap_y, gap_z = gap
        z_at = lax.rem(lane, HALF)
        inside = (
            (z_at < n)
            & (z_at + gap_z >= 0)
            & (z_at + gap_z < n)
            & (row + gap_x >= 0)
            & (row + gap_x < n)
        )
        for yo in range(half):
            s = gap_y + yo
            under = s < 0
            over = s >= half
            src = s + jnp.where(under, half, 0) - jnp.where(over, half, 0)
            tile = held_j[pl.ds(src * wide + half + gap_x, n), :]
            amount = (2 * LANES - gap_z + jnp.where(under | over, HALF, 0)) % LANES
            tile = pltpu.roll(tile, amount, 1)
            low_lane = jnp.where(under, HALF, 0)
            high_lane = jnp.where(over, HALF, LANES)
            good = inside & (lane >= low_lane) & (lane < high_lane)
            use(yo, jnp.where(good, tile, 0.0))

    def swapped(ref, at):
        a = ref[pl.ds(at, half, stride=n), :]
        b = ref[pl.ds(at + half, half, stride=n), :]
        top = jnp.where(left_half, a, pltpu.roll(b, HALF, 1))
        bottom = jnp.where(left_half, pltpu.roll(a, HALF, 1), b)
        return jnp.concatenate([top, bottom], axis=0)

    def task(which, carry):
        outgoing = which == 0

        def lister(k):
            return jnp.where(outgoing, mine[0, k], theirs[0, k])

        def source(k):
            return jnp.where(outgoing, theirs[0, k], mine[0, k])

        lister_group = jnp.where(outgoing, me, them)
        source_group = jnp.where(outgoing, them, me)
        listed = lister(at_count)
        i_at = jnp.int32(0)
        found = jnp.int32(0)
        for p in range(slots):
            hit = (lister(at_source + p) == source_group) & (p < listed)
            i_at = jnp.where(hit, lister(3 * orbs + p), i_at)
            found = jnp.where(hit, 1, found)
        j_at = source(at_pick + lister_group)
        gap = [lister(i_at * 3 + k) - source(j_at * 3 + k) for k in range(3)]

        @pl.when(found == 1)
        def _():
            @pl.when(which == 0)
            def _():
                dense_i[...] = own[i_at]
                for q in range(orbs):
                    @pl.when(j_at == q)
                    def _():
                        fetch(dense_j, q)

            @pl.when(which == 1)
            def _():
                dense_j[...] = own[j_at]
                for q in range(orbs):
                    @pl.when(i_at == q)
                    def _():
                        fetch(dense_i, q)

            def put_i(yo, tile):
                held_i[yo * n : (yo + 1) * n, :] = tile

            def put_j(yo, tile):
                held_j[yo * wide + half : yo * wide + half + n, :] = tile

            unpack(dense_i, put_i)
            unpack(dense_j, put_j)

            def use_moved(yo, tile):
                moved[yo * n : (yo + 1) * n, :] = tile

            shifted(gap, use_moved)
            lane_side = table[: 2 * LANES, : 2 * LANES].astype(bf16)
            row_side = table[2 * LANES :, : 4 * n].astype(bf16)
            modes = table.at[:, 2 * LANES :]
            rows = chunk * n
            for c in range(half // chunk):
                here = slice(c * rows, (c + 1) * rows)
                spectrum = lane_turn(held_i[here, :] * moved[here, :], lane_side)
                for q in range(0, chunk, 2):
                    pair = row_turn([spectrum[(q + k) * n : (q + k + 1) * n] for k in range(2)], row_side)
                    for k in range(2):
                        at = c * rows + (q + k) * n
                        field[at : at + n, :] = pair[k]
            for xo in range(0, half, 2):
                pair = row_turn([swapped(field, xo + k) for k in range(2)], row_side)
                pair = [pair[k] / (modes[:n, :] + modes[n + xo + k : n + xo + k + 1, :]) for k in range(2)]
                pair = row_turn(pair, row_side)
                for k in range(2):
                    other[(xo + k) * n : (xo + k + 1) * n, :] = pair[k]
            for c in range(half // chunk):
                tiles = []
                for q in range(0, chunk, 2):
                    tiles += row_turn([swapped(other, c * chunk + q + k) for k in range(2)], row_side)
                field[c * rows : (c + 1) * rows, :] = lane_turn(jnp.concatenate(tiles, axis=0), lane_side)

            @pl.when(which == 0)
            def _():
                for yo in range(half):
                    here = slice(yo * n, (yo + 1) * n)
                    there = pl.ds(i_at * (half * n) + yo * n, n)
                    total[there, :] += field[here, :] * moved[here, :]

            @pl.when(which == 1)
            def _():
                for yo in range(half):
                    here = slice(yo * n, (yo + 1) * n)
                    put_j(yo, (field[here, :] * held_i[here, :]).astype(bf16).astype(f32))

                def add_back(yo, tile):
                    there = pl.ds(j_at * (half * n) + yo * n, n)
                    total[there, :] += tile

                shifted([-k for k in gap], add_back)

        return carry

    lax.fori_loop(0, 2, task, 0)

    if last:
        for a in range(orbs):
            current = {}
            for yo in range(half):
                start = yo * n % LANES
                first_tile = yo * n // LANES
                tile = total[a * half * n + yo * n : a * half * n + (yo + 1) * n, :]
                for h in range(2):
                    t = first_tile + h * cells_tile
                    amount = (start - h * HALF) % LANES
                    piece = pltpu.roll(tile, amount, 1) if amount else tile
                    current[t] = jnp.where(lane >= start, piece, current[t]) if t in current else piece
                    if start + n >= LANES:
                        here = slice(t * LANES, (t + 1) * LANES)
                        if pieces:
                            flat[pl.ds(t * orbs * n + a, n, stride=orbs), :] = current.pop(t)
                        else:
                            outs[0][a, :, here] = current.pop(t).astype(bf16)
                        if start + n > LANES:
                            current[t + 1] = piece
        depth = n // pieces * orbs if pieces else 0
        tiles = n * n // LANES
        for k in range(pieces):
            at = jnp.bitwise_xor(member, k) * depth
            for t in range(tiles):
                outs[k][:, t * LANES : (t + 1) * LANES] = flat[pl.ds(t * orbs * n + at, 8), :].astype(bf16)
            for t in range(tiles // 2):
                tail = [flat[pl.ds((t + h * tiles // 2) * orbs * n + at + 8, 4), :] for h in range(2)]
                tail_at = (tiles + t) * LANES
                outs[k][:, tail_at : tail_at + LANES] = jnp.concatenate(tail, axis=0).astype(bf16)


def pack_kernel(groups, offsets, pick, pair_local, pair_source, pair_count, orbitals, *outs):
    *plain, box, mine = outs
    orbs, n, plane = orbitals.shape
    group = lax.axis_index("grp").astype(jnp.int32)
    member = lax.axis_index("dev").astype(jnp.int32)
    slots = pair_local.shape[2]
    numbers = [offsets[a, k] for a in range(orbs) for k in range(3)]
    numbers += [pair_local[0, 0, p] for p in range(slots)]
    numbers += [pair_source[0, 0, p] for p in range(slots)]
    numbers += [pair_count[0, 0, 0], group, member]
    numbers += [pick[0, g, member] for g in range(groups)]
    lane = lax.broadcasted_iota(jnp.int32, (ROWS, LANES), 1)
    row = jnp.zeros((ROWS, LANES), jnp.int32)
    for k, number in enumerate(numbers):
        mine[0, k] = number
        row = jnp.where(lane == k, number, row)
    for q in range(orbs - 1):
        plain[q][...] = orbitals[q]
    for r in range(n // ROWS):
        box[:, r * plane : (r + 1) * plane] = orbitals[orbs - 1, r * ROWS : (r + 1) * ROWS, :]
    box[:, n * plane // ROWS :] = row.astype(f32).astype(bf16)


def pair_step(step, pieces, first, last, mine, own, others, table, total):
    orbs, n, plane = own.shape
    half = n // 2
    slots = pieces[1]
    pieces = pieces[0] if last else 0
    vmem = pl.BlockSpec(memory_space=pltpu.VMEM)
    smem = pl.BlockSpec(memory_space=pltpu.SMEM)
    operands = [mine, own, *others, table]
    specs = [smem] + [vmem] * (2 + orbs)
    if not first:
        operands.append(total)
        specs.append(vmem)
    held = jax.ShapeDtypeStruct((orbs * half * n, LANES), f32)
    rows = half * n
    scratch = [
        pltpu.VMEM((n, plane), bf16),
        pltpu.VMEM((n, plane), bf16),
        pltpu.VMEM((rows, LANES), f32),
        pltpu.VMEM((half * (n + 2 * half), LANES), f32),
        pltpu.VMEM((rows, LANES), f32),
        pltpu.VMEM((rows, LANES), f32),
        pltpu.VMEM((rows, LANES), f32),
        pltpu.SMEM(mine.shape, jnp.int32),
    ]
    shapes = held
    if last:
        shapes = jax.ShapeDtypeStruct(own.shape, bf16)
        if pieces:
            scratch.insert(0, pltpu.VMEM((orbs * n * plane // LANES, LANES), f32))
            shapes = [jax.ShapeDtypeStruct((8, orbs * n * plane // pieces // 8), bf16)] * pieces
        scratch.insert(0, pltpu.VMEM(held.shape, f32))
    return pl.pallas_call(
        functools.partial(pair_kernel, (n, orbs, slots), pieces, first, last),
        out_shape=shapes,
        in_specs=specs,
        out_specs=[vmem] * pieces if pieces else vmem,
        scratch_shapes=scratch,
        compiler_params=pltpu.CompilerParams(vmem_limit_bytes=32 << 20),
        cost_estimate=pl.CostEstimate(flops=2 * 12 * 3 * n**4, bytes_accessed=4 * n**3 * 4, transcendentals=0),
        name=f"pairs_{step}",
    )(*operands)


def gather_kernel(n, orbs, member_ref, *refs):
    devices = len(refs) - 3
    out, rows, mixed = refs[devices:]
    tiles = n * n // LANES
    member = member_ref[0]
    for k in range(devices):
        at = pl.multiple_of(jnp.bitwise_xor(member, k) * 8, 8)
        for t in range(tiles * 3 // 2):
            rows[pl.ds(t * devices * 8 + at, 8), :] = refs[k][:, t * LANES : (t + 1) * LANES].astype(f32)
    for x in range(n // devices):
        for t in range(tiles):
            here = slice((x * tiles + t) * LANES, (x * tiles + t + 1) * LANES)
            at = (x * tiles + t) * orbs * devices
            for a in range(orbs):
                q = x * orbs + a
                tile = t
                if q >= 8:
                    q += 4 * (t * 2 // tiles) - 8
                    tile = tiles + t % (tiles // 2)
                mixed[pl.ds(at + a, devices, stride=orbs), :] = rows[
                    pl.ds(tile * devices * 8 + q, devices, stride=8), :
                ]
            out[:, here] = mixed[at : at + orbs * devices, :]


def body(orbitals, offsets, pick, pair_local, pair_source, pair_count):
    orbs, n, plane = orbitals.shape
    groups = lax.axis_size("grp")
    devices = lax.axis_size("dev")
    member = lax.axis_index("dev").astype(jnp.int32)
    slots = pair_local.shape[2]
    vmem = pl.BlockSpec(memory_space=pltpu.VMEM)
    smem = pl.BlockSpec(memory_space=pltpu.SMEM)
    table = jnp.asarray(np_tables(n))
    numbers = 3 * orbs + 2 * slots + 3 + groups
    *held, mine = pl.pallas_call(
        functools.partial(pack_kernel, groups),
        out_shape=[jax.ShapeDtypeStruct((n, plane), bf16)] * (orbs - 1)
        + [
            jax.ShapeDtypeStruct((ROWS, n * plane // ROWS + LANES), bf16),
            jax.ShapeDtypeStruct((1, numbers), jnp.int32),
        ],
        in_specs=[smem] * 4 + [vmem] * 2,
        out_specs=[vmem] * orbs + [smem],
        name="pack",
    )(offsets, pick.transpose(0, 2, 1), pair_local, pair_source, pair_count, orbitals)
    by_pieces = devices & (devices - 1) == 0 and n % devices == 0 and n // devices * orbs == 12
    pieces = devices if by_pieces else 0
    ring = [(g, (g + 1) % groups) for g in range(groups)]
    total = None
    for step in range(1, groups):
        held = [lax.ppermute(h, "grp", ring) for h in held]
        for q in range(orbs):
            held[q], _ = lax.optimization_barrier((held[q], total))
        total = pair_step(
            step,
            (pieces, slots),
            step == 1,
            step == groups - 1,
            mine,
            orbitals,
            held,
            table,
            total,
        )
    if not pieces:
        whole = total.reshape(orbs, n * plane)
        return lax.all_to_all(whole, "dev", split_axis=1, concat_axis=0, tiled=True).astype(f32)
    arrived = [total[0]]
    for k in range(1, devices):
        arrived.append(lax.ppermute(total[k], "dev", [(d, d ^ k) for d in range(devices)]))
    return pl.pallas_call(
        functools.partial(gather_kernel, n, orbs),
        out_shape=jax.ShapeDtypeStruct((orbs * devices, n * plane // devices), f32),
        in_specs=[smem] + [vmem] * devices,
        out_specs=vmem,
        scratch_shapes=[pltpu.VMEM((orbs * n * plane // LANES, LANES), f32)] * 2,
        compiler_params=pltpu.CompilerParams(vmem_limit_bytes=32 << 20),
        name="cells",
    )(member.reshape(1), *arrived)


def solution(mesh):
    return jax.shard_map(
        body,
        mesh=mesh,
        in_specs=(
            P(("grp", "dev"), None, None),
            P(("grp", "dev"), None),
            P("grp", None, None),
            P("grp", "dev", None),
            P("grp", "dev", None),
            P("grp", "dev", None),
        ),
        out_specs=P("grp", "dev"),
        check_vma=False,
    )
```

```python
import functools
import math

import numpy as np

import jax
import jax.numpy as jnp
from jax import lax
from jax.experimental import pallas as pl
from jax.experimental.pallas import tpu as pltpu
from jax.sharding import PartitionSpec as P

LANES = 128
HALF = 64
ROWS = 16
f32 = jnp.float32
bf16 = jnp.bfloat16


def np_tables(n):
    freq = np.arange(n)
    step = math.pi / (n + 1)
    sine = math.sqrt(2.0 / (n + 1)) * np.sin(step * ((freq[:, None] + 1) * (freq[None, :] + 1) % (2 * (n + 1))))
    sine = sine.astype(np.float32)
    high = sine.astype(jnp.bfloat16)
    low = (sine - high.astype(np.float32)).astype(jnp.bfloat16)

    def two(block):
        out = np.zeros((LANES, LANES), jnp.bfloat16)
        out[:n, :n] = block
        out[HALF : HALF + n, HALF : HALF + n] = block
        return out

    lane_side = np.block([[two(high), two(low)], [two(high), two(low)]])
    row_side = np.concatenate([high, high, low, 0 * low], axis=1)
    modes = (2.0 - 2.0 * np.cos(step * (freq + 1.0))).astype(np.float32)
    base = np.ones((n, LANES), np.float32)
    outer = np.ones((n // 2, LANES), np.float32)
    for half in range(2):
        at = half * HALF
        base[:, at : at + n] = modes[:, None] + modes[None, :]
        outer[:, at : at + HALF] = modes[half * (n // 2) : (half + 1) * (n // 2), None]
    pad = np.zeros((n, 2 * LANES - 4 * n), jnp.bfloat16)
    sines = np.concatenate([lane_side, np.concatenate([row_side, pad], axis=1)]).astype(np.float32)
    modes = np.concatenate([base, outer])
    modes = np.pad(modes, ((0, len(sines) - len(modes)), (0, 0)))
    return np.concatenate([sines, modes], axis=1)


def split(x):
    high = x.astype(bf16)
    return high, (x - high.astype(f32)).astype(bf16)


def lane_turn(x, lane_side):
    both = jnp.concatenate(split(x), axis=1)
    out = jnp.dot(both, lane_side, preferred_element_type=f32)
    return out[:, :LANES] + out[:, LANES:]


def row_turn(tiles, row_side):
    columns = []
    for tile in tiles:
        high, low = split(tile)
        columns.append(jnp.concatenate([high, low, high], axis=0))
    out = jnp.dot(row_side, jnp.concatenate(columns, axis=1), preferred_element_type=f32)
    return out[:, :LANES], out[:, LANES:]


def unpack(dense, put):
    n = dense.shape[0]
    half = n // 2
    lane = lax.broadcasted_iota(jnp.int32, (n, LANES), 1)
    for yo in range(half):
        start = yo * n % LANES
        halves = []
        for h in range(2):
            t = (yo * n // LANES + h * (half * n // LANES)) * LANES
            piece = dense[:, t : t + LANES].astype(f32)
            if start + n > LANES:
                after = dense[:, t + LANES : t + 2 * LANES].astype(f32)
                piece = jnp.where(lane >= start, piece, after)
            amount = (h * HALF - start) % LANES
            halves.append(pltpu.roll(piece, amount, 1) if amount else piece)
        put(yo, jnp.where(lane < HALF, halves[0], halves[1]))


def setup_kernel(own, table, mine, held, sines, modes, total):
    orbs, n, _ = own.shape
    half = n // 2
    wide = n + 2 * half
    for q in range(orbs):

        def put(yo, tile, q=q):
            at = (q * half + yo) * wide + half
            held[at : at + n, :] = tile

        unpack(own.at[q], put)
    sines[...] = table[:, : 2 * LANES].astype(bf16)
    modes[...] = table[: modes.shape[0], 2 * LANES :]
    total[...] = jnp.zeros_like(total)


def pair_kernel(sizes, pieces, tasks, last, *refs):
    n, orbs, slots = sizes
    half = n // 2
    cells_tile = half * n // LANES
    wide = n + 2 * half
    mine, own, sines, modes = refs[:4]
    others = refs[4 : 4 + orbs]
    total_in = refs[4 + orbs]
    rest = list(refs[5 + orbs :])
    if last:
        outs = [rest.pop(0) for _ in range(max(pieces, 1))]
        total = rest.pop(0)
        flat = rest.pop(0) if pieces else None
    else:
        total = rest.pop(0)
    dense, held, moved, field, other, theirs = rest
    lists = others[-1][:, n * n * n // ROWS :].astype(f32).astype(jnp.int32)
    for k in range(mine.shape[1]):
        theirs[0, k] = lists[0, k]

    def fetch(q):
        if q < orbs - 1:
            dense[...] = others[q][...]
        else:
            for r in range(n // ROWS):
                dense[r * ROWS : (r + 1) * ROWS, :] = others[q][:, r * n * n : (r + 1) * n * n]

    lane = lax.broadcasted_iota(jnp.int32, (n, LANES), 1)
    row = lax.broadcasted_iota(jnp.int32, (n, LANES), 0)
    left_half = lane[:half] < HALF
    total[...] = total_in[...]

    at_source = 3 * orbs + slots
    at_count = at_source + slots
    at_group = at_count + 1
    at_pick = at_group + 2
    member = mine[0, at_group + 1]

    def tile_at(base, yo):
        return pl.ds(base + yo * wide + half, n)

    def shifted(ref, base, gap, use):
        gap_x, gap_y, gap_z = gap
        z_at = lax.rem(lane, HALF)
        inside = (
            (z_at < n)
            & (z_at + gap_z >= 0)
            & (z_at + gap_z < n)
            & (row + gap_x >= 0)
            & (row + gap_x < n)
        )
        for yo in range(half):
            s = gap_y + yo
            under = s < 0
            over = s >= half
            src = s + jnp.where(under, half, 0) - jnp.where(over, half, 0)
            tile = ref[pl.ds(base + src * wide + half + gap_x, n), :]
            amount = (2 * LANES - gap_z + jnp.where(under | over, HALF, 0)) % LANES
            tile = pltpu.roll(tile, amount, 1)
            low_lane = jnp.where(under, HALF, 0)
            high_lane = jnp.where(over, HALF, LANES)
            good = inside & (lane >= low_lane) & (lane < high_lane)
            use(yo, jnp.where(good, tile, 0.0))

    def swapped(ref, at):
        a = ref[pl.ds(at, half, stride=n), :]
        b = ref[pl.ds(at + half, half, stride=n), :]
        top = jnp.where(left_half, a, pltpu.roll(b, HALF, 1))
        bottom = jnp.where(left_half, pltpu.roll(a, HALF, 1), b)
        return jnp.concatenate([top, bottom], axis=0)

    def rows_of(ref, at):
        return ref[at * n : (at + 1) * n, :]

    def task(outgoing):
        lister, source = (mine, theirs) if outgoing else (theirs, mine)
        source_group = source[0, at_group]
        listed = lister[0, at_count]
        i_at = jnp.int32(0)
        found = jnp.int32(0)
        for p in range(slots):
            hit = (lister[0, at_source + p] == source_group) & (p < listed)
            i_at = jnp.where(hit, lister[0, 3 * orbs + p], i_at)
            found = jnp.where(hit, 1, found)
        j_at = source[0, at_pick + lister[0, at_group]]
        gap = [lister[0, i_at * 3 + k] - source[0, j_at * 3 + k] for k in range(3)]
        own_at, other_at = (i_at, j_at) if outgoing else (j_at, i_at)
        base = own_at * (half * wide)
        box_i, base_i, box_j, base_j = (own, base, held, 0) if outgoing else (held, 0, own, base)

        @pl.when(found == 1)
        def _():
            for q in range(orbs):
                @pl.when(other_at == q)
                def _():
                    fetch(q)

            def put(yo, tile):
                held[tile_at(0, yo), :] = tile

            unpack(dense, put)

            def use_moved(yo, tile):
                moved[yo * n : (yo + 1) * n, :] = tile
                field[yo * n : (yo + 1) * n, :] = box_i[tile_at(base_i, yo), :] * tile

            shifted(box_j, base_j, gap, use_moved)
            lane_side = sines[: 2 * LANES, :]
            row_side = sines[2 * LANES :, : 3 * n]
            other[...] = lane_turn(field[...], lane_side)
            for at in range(0, half, 2):
                pair = row_turn([rows_of(other, at + k) for k in range(2)], row_side)
                for k in range(2):
                    field[(at + k) * n : (at + k + 1) * n, :] = pair[k]
            for at in range(0, half, 2):
                pair = row_turn([swapped(field, at + k) for k in range(2)], row_side)
                pair = [pair[k] / (modes[:n, :] + modes[n + at + k : n + at + k + 1, :]) for k in range(2)]
                pair = row_turn(pair, row_side)
                for k in range(2):
                    other[(at + k) * n : (at + k + 1) * n, :] = pair[k]
            for at in range(0, half, 2):
                pair = row_turn([swapped(other, at + k) for k in range(2)], row_side)
                for k in range(2):
                    field[(at + k) * n : (at + k + 1) * n, :] = pair[k]
            field[...] = lane_turn(field[...], lane_side)

            if outgoing:
                for yo in range(half):
                    there = pl.ds(own_at * (half * n) + yo * n, n)
                    total[there, :] += rows_of(field, yo) * rows_of(moved, yo)
            else:
                for yo in range(half):
                    term = rows_of(field, yo) * held[tile_at(0, yo), :]
                    held[tile_at(0, yo), :] = term.astype(bf16).astype(f32)

                def add_back(yo, tile):
                    there = pl.ds(own_at * (half * n) + yo * n, n)
                    total[there, :] += tile

                shifted(held, 0, [-k for k in gap], add_back)

    for outgoing in tasks:
        task(outgoing)

    if last:
        for a in range(orbs):
            current = {}
            for yo in range(half):
                start = yo * n % LANES
                first_tile = yo * n // LANES
                tile = total[a * half * n + yo * n : a * half * n + (yo + 1) * n, :]
                for h in range(2):
                    t = first_tile + h * cells_tile
                    amount = (start - h * HALF) % LANES
                    piece = pltpu.roll(tile, amount, 1) if amount else tile
                    current[t] = jnp.where(lane >= start, piece, current[t]) if t in current else piece
                    if start + n >= LANES:
                        here = slice(t * LANES, (t + 1) * LANES)
                        if pieces:
                            flat[pl.ds(t * orbs * n + a, n, stride=orbs), :] = current.pop(t)
                        else:
                            outs[0][a, :, here] = current.pop(t).astype(bf16)
                        if start + n > LANES:
                            current[t + 1] = piece
        depth = n // pieces * orbs if pieces else 0
        tiles = n * n // LANES
        for k in range(pieces):
            at = jnp.bitwise_xor(member, k) * depth
            for t in range(tiles):
                outs[k][:, t * LANES : (t + 1) * LANES] = flat[pl.ds(t * orbs * n + at, 8), :].astype(bf16)
            for t in range(tiles // 2):
                tail = [flat[pl.ds((t + h * tiles // 2) * orbs * n + at + 8, 4), :] for h in range(2)]
                tail_at = (tiles + t) * LANES
                outs[k][:, tail_at : tail_at + LANES] = jnp.concatenate(tail, axis=0).astype(bf16)


def pack_kernel(groups, offsets, pick, pair_local, pair_source, pair_count, orbitals, *outs):
    *plain, box, mine = outs
    orbs, n, plane = orbitals.shape
    group = lax.axis_index("grp").astype(jnp.int32)
    member = lax.axis_index("dev").astype(jnp.int32)
    slots = pair_local.shape[2]
    numbers = [offsets[a, k] for a in range(orbs) for k in range(3)]
    numbers += [pair_local[0, 0, p] for p in range(slots)]
    numbers += [pair_source[0, 0, p] for p in range(slots)]
    numbers += [pair_count[0, 0, 0], group, member]
    numbers += [pick[0, g, member] for g in range(groups)]
    lane = lax.broadcasted_iota(jnp.int32, (ROWS, LANES), 1)
    row = jnp.zeros((ROWS, LANES), jnp.int32)
    for k, number in enumerate(numbers):
        mine[0, k] = number
        row = jnp.where(lane == k, number, row)
    for q in range(orbs - 1):
        plain[q][...] = orbitals[q]
    for r in range(n // ROWS):
        box[:, r * plane : (r + 1) * plane] = orbitals[orbs - 1, r * ROWS : (r + 1) * ROWS, :]
    box[:, n * plane // ROWS :] = row.astype(f32).astype(bf16)


def setup(own, table, mine):
    orbs, n, _ = own.shape
    half = n // 2
    vmem = pl.BlockSpec(memory_space=pltpu.VMEM)
    return pl.pallas_call(
        setup_kernel,
        out_shape=[
            jax.ShapeDtypeStruct((orbs * half * (n + 2 * half), LANES), f32),
            jax.ShapeDtypeStruct((table.shape[0], 2 * LANES), bf16),
            jax.ShapeDtypeStruct((n + half, LANES), f32),
            jax.ShapeDtypeStruct((orbs * half * n, LANES), f32),
        ],
        in_specs=[vmem, vmem, pl.BlockSpec(memory_space=pltpu.SMEM)],
        out_specs=[vmem] * 4,
        compiler_params=pltpu.CompilerParams(vmem_limit_bytes=16 << 20),
        name="setup",
    )(own, table, mine)


def pair_step(name, n, slots, pieces, tasks, last, mine, own, sines, modes, others, total):
    orbs = len(others)
    plane = n * n
    half = n // 2
    pieces = pieces if last else 0
    vmem = pl.BlockSpec(memory_space=pltpu.VMEM)
    smem = pl.BlockSpec(memory_space=pltpu.SMEM)
    held = jax.ShapeDtypeStruct(total.shape, f32)
    rows = half * n
    scratch = [
        pltpu.VMEM((n, plane), bf16),
        pltpu.VMEM((half * (n + 2 * half), LANES), f32),
        pltpu.VMEM((rows, LANES), f32),
        pltpu.VMEM((rows, LANES), f32),
        pltpu.VMEM((rows, LANES), f32),
        pltpu.SMEM(mine.shape, jnp.int32),
    ]
    shapes = held
    if last:
        shapes = jax.ShapeDtypeStruct((orbs, n, plane), bf16)
        if pieces:
            scratch.insert(0, pltpu.VMEM((orbs * n * plane // LANES, LANES), f32))
            shapes = [jax.ShapeDtypeStruct((8, orbs * n * plane // pieces // 8), bf16)] * pieces
        scratch.insert(0, pltpu.VMEM(held.shape, f32))
    return pl.pallas_call(
        functools.partial(pair_kernel, (n, orbs, slots), pieces, tasks, last),
        out_shape=shapes,
        in_specs=[smem] + [vmem] * (4 + orbs),
        out_specs=[vmem] * pieces if pieces else vmem,
        scratch_shapes=scratch,
        input_output_aliases={} if last else {4 + orbs: 0},
        compiler_params=pltpu.CompilerParams(vmem_limit_bytes=32 << 20),
        cost_estimate=pl.CostEstimate(flops=2 * 12 * 3 * n**4, bytes_accessed=4 * n**3 * 4, transcendentals=0),
        name=name,
    )(mine, own, sines, modes, *others, total)


def gather_kernel(n, orbs, member_ref, *refs):
    devices = len(refs) - 3
    out, rows, mixed = refs[devices:]
    tiles = n * n // LANES
    member = member_ref[0]
    for k in range(devices):
        at = pl.multiple_of(jnp.bitwise_xor(member, k) * 8, 8)
        for t in range(tiles * 3 // 2):
            rows[pl.ds(t * devices * 8 + at, 8), :] = refs[k][:, t * LANES : (t + 1) * LANES].astype(f32)
    for x in range(n // devices):
        for t in range(tiles):
            here = slice((x * tiles + t) * LANES, (x * tiles + t + 1) * LANES)
            at = (x * tiles + t) * orbs * devices
            for a in range(orbs):
                q = x * orbs + a
                tile = t
                if q >= 8:
                    q += 4 * (t * 2 // tiles) - 8
                    tile = tiles + t % (tiles // 2)
                mixed[pl.ds(at + a, devices, stride=orbs), :] = rows[
                    pl.ds(tile * devices * 8 + q, devices, stride=8), :
                ]
            out[:, here] = mixed[at : at + orbs * devices, :]


def body(orbitals, offsets, pick, pair_local, pair_source, pair_count):
    orbs, n, plane = orbitals.shape
    groups = lax.axis_size("grp")
    devices = lax.axis_size("dev")
    member = lax.axis_index("dev").astype(jnp.int32)
    slots = pair_local.shape[2]
    vmem = pl.BlockSpec(memory_space=pltpu.VMEM)
    smem = pl.BlockSpec(memory_space=pltpu.SMEM)
    table = jnp.asarray(np_tables(n))
    numbers = 3 * orbs + 2 * slots + 3 + groups
    *held, mine = pl.pallas_call(
        functools.partial(pack_kernel, groups),
        out_shape=[jax.ShapeDtypeStruct((n, plane), bf16)] * (orbs - 1)
        + [
            jax.ShapeDtypeStruct((ROWS, n * plane // ROWS + LANES), bf16),
            jax.ShapeDtypeStruct((1, numbers), jnp.int32),
        ],
        in_specs=[smem] * 4 + [vmem] * 2,
        out_specs=[vmem] * orbs + [smem],
        name="pack",
    )(offsets, pick.transpose(0, 2, 1), pair_local, pair_source, pair_count, orbitals)
    by_pieces = devices & (devices - 1) == 0 and n % devices == 0 and n // devices * orbs == 12
    pieces = devices if by_pieces else 0
    ring = [(g, (g + 1) % groups) for g in range(groups)]
    own, sines, modes, total = setup(orbitals, table, mine)
    early = [total] * orbs
    for step in range(1, groups):
        last = step == groups - 1
        held = [lax.ppermute(h, "grp", ring) for h in held]
        for q in range(orbs):
            held[q], _ = lax.optimization_barrier((held[q], early[q]))
        early = []
        for tasks in [(True, False)] if last else [(True,), (False,)]:
            name = f"pairs_{step}_{len(early)}"
            total = pair_step(name, n, slots, pieces, tasks, last, mine, own, sines, modes, held, total)
            early.insert(0, total)
        early = [early[0]] * (orbs - 1) + early[-1:]
    if not pieces:
        whole = total.reshape(orbs, n * plane)
        return lax.all_to_all(whole, "dev", split_axis=1, concat_axis=0, tiled=True).astype(f32)
    arrived = [total[0]]
    for k in range(1, devices):
        arrived.append(lax.ppermute(total[k], "dev", [(d, d ^ k) for d in range(devices)]))
    return pl.pallas_call(
        functools.partial(gather_kernel, n, orbs),
        out_shape=jax.ShapeDtypeStruct((orbs * devices, n * plane // devices), f32),
        in_specs=[smem] + [vmem] * devices,
        out_specs=vmem,
        scratch_shapes=[pltpu.VMEM((orbs * n * plane // LANES, LANES), f32)] * 2,
        compiler_params=pltpu.CompilerParams(vmem_limit_bytes=32 << 20),
        name="cells",
    )(member.reshape(1), *arrived)


def solution(mesh):
    return jax.shard_map(
        body,
        mesh=mesh,
        in_specs=(
            P(("grp", "dev"), None, None),
            P(("grp", "dev"), None),
            P("grp", None, None),
            P("grp", "dev", None),
            P("grp", "dev", None),
            P("grp", "dev", None),
        ),
        out_specs=P("grp", "dev"),
        check_vma=False,
    )
```

```python
import functools
import math

import numpy as np

import jax
import jax.numpy as jnp
from jax import lax
from jax.experimental import pallas as pl
from jax.experimental.pallas import tpu as pltpu
from jax.sharding import PartitionSpec as P

LANES = 128
HALF = 64
ROWS = 16
f32 = jnp.float32
bf16 = jnp.bfloat16


def np_tables(n):
    freq = np.arange(n)
    step = math.pi / (n + 1)
    sine = math.sqrt(2.0 / (n + 1)) * np.sin(step * ((freq[:, None] + 1) * (freq[None, :] + 1) % (2 * (n + 1))))
    sine = sine.astype(np.float32)
    high = sine.astype(jnp.bfloat16)
    low = (sine - high.astype(np.float32)).astype(jnp.bfloat16)

    def two(block):
        out = np.zeros((LANES, LANES), jnp.bfloat16)
        out[:n, :n] = block
        out[HALF : HALF + n, HALF : HALF + n] = block
        return out

    lane_side = np.block([[two(high), two(low)], [two(high), two(low)]])
    row_side = np.concatenate([high, high, low, 0 * low], axis=1)
    modes = (2.0 - 2.0 * np.cos(step * (freq + 1.0))).astype(np.float32)
    base = np.ones((n, LANES), np.float32)
    outer = np.ones((n // 2, LANES), np.float32)
    for half in range(2):
        at = half * HALF
        base[:, at : at + n] = modes[:, None] + modes[None, :]
        outer[:, at : at + HALF] = modes[half * (n // 2) : (half + 1) * (n // 2), None]
    pad = np.zeros((n, 2 * LANES - 4 * n), jnp.bfloat16)
    sines = np.concatenate([lane_side, np.concatenate([row_side, pad], axis=1)]).astype(np.float32)
    modes = np.concatenate([base, outer])
    modes = np.pad(modes, ((0, len(sines) - len(modes)), (0, 0)))
    return np.concatenate([sines, modes], axis=1)


def split(x):
    high = x.astype(bf16)
    return high, (x - high.astype(f32)).astype(bf16)


def lane_turn(x, lane_side):
    both = jnp.concatenate(split(x), axis=1)
    out = jnp.dot(both, lane_side, preferred_element_type=f32)
    return out[:, :LANES] + out[:, LANES:]


def row_turn(tiles, row_side):
    columns = []
    for tile in tiles:
        high, low = split(tile)
        columns.append(jnp.concatenate([high, low, high], axis=0))
    out = jnp.dot(row_side, jnp.concatenate(columns, axis=1), preferred_element_type=f32)
    return [out[:, k * LANES : (k + 1) * LANES] for k in range(len(tiles))]


def unpack(dense, put):
    n = dense.shape[0]
    half = n // 2
    lane = lax.broadcasted_iota(jnp.int32, (n, LANES), 1)
    for yo in range(half):
        start = yo * n % LANES
        halves = []
        for h in range(2):
            t = (yo * n // LANES + h * (half * n // LANES)) * LANES
            piece = dense[:, t : t + LANES].astype(f32)
            if start + n > LANES:
                after = dense[:, t + LANES : t + 2 * LANES].astype(f32)
                piece = jnp.where(lane >= start, piece, after)
            amount = (h * HALF - start) % LANES
            halves.append(pltpu.roll(piece, amount, 1) if amount else piece)
        put(yo, jnp.where(lane < HALF, halves[0], halves[1]))


def setup_kernel(own, table, mine, held, sines, modes, total):
    orbs, n, _ = own.shape
    half = n // 2
    wide = n + 2 * half
    for q in range(orbs):

        def put(yo, tile, q=q):
            at = (q * half + yo) * wide + half
            held[at : at + n, :] = tile

        unpack(own.at[q], put)
    sines[...] = table[:, : 2 * LANES].astype(bf16)
    modes[...] = table[: modes.shape[0], 2 * LANES :]
    total[...] = jnp.zeros_like(total)


def pair_kernel(sizes, pieces, tasks, last, *refs):
    n, orbs, slots = sizes
    half = n // 2
    cells_tile = half * n // LANES
    wide = n + 2 * half
    mine, own, sines, modes = refs[:4]
    others = refs[4 : 4 + orbs]
    total_in = refs[4 + orbs]
    rest = list(refs[5 + orbs :])
    if last:
        outs = [rest.pop(0) for _ in range(max(pieces, 1))]
        total = rest.pop(0)
        flat = rest.pop(0) if pieces else None
    else:
        total = rest.pop(0)
    dense, held, moved, field, other, theirs = rest
    lists = others[-1][:, n * n * n // ROWS :].astype(f32).astype(jnp.int32)
    for k in range(mine.shape[1]):
        theirs[0, k] = lists[0, k]

    def fetch(q):
        if q < orbs - 1:
            dense[...] = others[q][...]
        else:
            for r in range(n // ROWS):
                dense[r * ROWS : (r + 1) * ROWS, :] = others[q][:, r * n * n : (r + 1) * n * n]

    lane = lax.broadcasted_iota(jnp.int32, (n, LANES), 1)
    row = lax.broadcasted_iota(jnp.int32, (n, LANES), 0)
    left_half = lane[:half] < HALF
    total[...] = total_in[...]

    at_source = 3 * orbs + slots
    at_count = at_source + slots
    at_group = at_count + 1
    at_pick = at_group + 2
    member = mine[0, at_group + 1]

    def tile_at(base, yo):
        return pl.ds(base + yo * wide + half, n)

    def shifted(ref, base, gap, use):
        gap_x, gap_y, gap_z = gap
        z_at = lax.rem(lane, HALF)
        inside = (
            (z_at < n)
            & (z_at + gap_z >= 0)
            & (z_at + gap_z < n)
            & (row + gap_x >= 0)
            & (row + gap_x < n)
        )
        for yo in range(half):
            s = gap_y + yo
            under = s < 0
            over = s >= half
            src = s + jnp.where(under, half, 0) - jnp.where(over, half, 0)
            tile = ref[pl.ds(base + src * wide + half + gap_x, n), :]
            amount = (2 * LANES - gap_z + jnp.where(under | over, HALF, 0)) % LANES
            tile = pltpu.roll(tile, amount, 1)
            low_lane = jnp.where(under, HALF, 0)
            high_lane = jnp.where(over, HALF, LANES)
            good = inside & (lane >= low_lane) & (lane < high_lane)
            use(yo, jnp.where(good, tile, 0.0))

    def swapped(ref, at):
        a = ref[pl.ds(at, half, stride=n), :]
        b = ref[pl.ds(at + half, half, stride=n), :]
        top = jnp.where(left_half, a, pltpu.roll(b, HALF, 1))
        bottom = jnp.where(left_half, pltpu.roll(a, HALF, 1), b)
        return jnp.concatenate([top, bottom], axis=0)

    def rows_of(ref, at):
        return ref[at * n : (at + 1) * n, :]

    def task(outgoing):
        lister, source = (mine, theirs) if outgoing else (theirs, mine)
        source_group = source[0, at_group]
        listed = lister[0, at_count]
        i_at = jnp.int32(0)
        found = jnp.int32(0)
        for p in range(slots):
            hit = (lister[0, at_source + p] == source_group) & (p < listed)
            i_at = jnp.where(hit, lister[0, 3 * orbs + p], i_at)
            found = jnp.where(hit, 1, found)
        j_at = source[0, at_pick + lister[0, at_group]]
        gap = [lister[0, i_at * 3 + k] - source[0, j_at * 3 + k] for k in range(3)]
        own_at, other_at = (i_at, j_at) if outgoing else (j_at, i_at)
        base = own_at * (half * wide)
        box_i, base_i, box_j, base_j = (own, base, held, 0) if outgoing else (held, 0, own, base)

        @pl.when(found == 1)
        def _():
            for q in range(orbs):
                @pl.when(other_at == q)
                def _():
                    fetch(q)

            def put(yo, tile):
                held[tile_at(0, yo), :] = tile

            unpack(dense, put)

            def use_moved(yo, tile):
                moved[yo * n : (yo + 1) * n, :] = tile
                field[yo * n : (yo + 1) * n, :] = box_i[tile_at(base_i, yo), :] * tile

            shifted(box_j, base_j, gap, use_moved)
            lane_side = sines[: 2 * LANES, :]
            row_side = sines[2 * LANES :, : 3 * n]
            other[...] = lane_turn(field[...], lane_side)
            tiles = row_turn([rows_of(other, at) for at in range(half)], row_side)
            for at in range(half):
                field[at * n : (at + 1) * n, :] = tiles[at]
            tiles = row_turn([swapped(field, at) for at in range(half)], row_side)
            tiles = [tiles[at] / (modes[:n, :] + modes[n + at : n + at + 1, :]) for at in range(half)]
            tiles = row_turn(tiles, row_side)
            for at in range(half):
                other[at * n : (at + 1) * n, :] = tiles[at]
            tiles = row_turn([swapped(other, at) for at in range(half)], row_side)
            for at in range(half):
                field[at * n : (at + 1) * n, :] = tiles[at]
            field[...] = lane_turn(field[...], lane_side)

            if outgoing:
                for yo in range(half):
                    there = pl.ds(own_at * (half * n) + yo * n, n)
                    total[there, :] += rows_of(field, yo) * rows_of(moved, yo)
            else:
                for yo in range(half):
                    term = rows_of(field, yo) * held[tile_at(0, yo), :]
                    held[tile_at(0, yo), :] = term.astype(bf16).astype(f32)

                def add_back(yo, tile):
                    there = pl.ds(own_at * (half * n) + yo * n, n)
                    total[there, :] += tile

                shifted(held, 0, [-k for k in gap], add_back)

    for outgoing in tasks:
        task(outgoing)

    if last:
        for a in range(orbs):
            current = {}
            for yo in range(half):
                start = yo * n % LANES
                first_tile = yo * n // LANES
                tile = total[a * half * n + yo * n : a * half * n + (yo + 1) * n, :]
                for h in range(2):
                    t = first_tile + h * cells_tile
                    amount = (start - h * HALF) % LANES
                    piece = pltpu.roll(tile, amount, 1) if amount else tile
                    current[t] = jnp.where(lane >= start, piece, current[t]) if t in current else piece
                    if start + n >= LANES:
                        here = slice(t * LANES, (t + 1) * LANES)
                        if pieces:
                            flat[pl.ds(t * orbs * n + a, n, stride=orbs), :] = current.pop(t)
                        else:
                            outs[0][a, :, here] = current.pop(t).astype(bf16)
                        if start + n > LANES:
                            current[t + 1] = piece
        depth = n // pieces * orbs if pieces else 0
        tiles = n * n // LANES
        for k in range(pieces):
            at = jnp.bitwise_xor(member, k) * depth
            for t in range(tiles):
                outs[k][:, t * LANES : (t + 1) * LANES] = flat[pl.ds(t * orbs * n + at, 8), :].astype(bf16)
            for t in range(tiles // 2):
                tail = [flat[pl.ds((t + h * tiles // 2) * orbs * n + at + 8, 4), :] for h in range(2)]
                tail_at = (tiles + t) * LANES
                outs[k][:, tail_at : tail_at + LANES] = jnp.concatenate(tail, axis=0).astype(bf16)


def pack_kernel(groups, offsets, pick, pair_local, pair_source, pair_count, orbitals, *outs):
    *plain, box, mine = outs
    orbs, n, plane = orbitals.shape
    group = lax.axis_index("grp").astype(jnp.int32)
    member = lax.axis_index("dev").astype(jnp.int32)
    slots = pair_local.shape[2]
    numbers = [offsets[a, k] for a in range(orbs) for k in range(3)]
    numbers += [pair_local[0, 0, p] for p in range(slots)]
    numbers += [pair_source[0, 0, p] for p in range(slots)]
    numbers += [pair_count[0, 0, 0], group, member]
    numbers += [pick[0, g, member] for g in range(groups)]
    lane = lax.broadcasted_iota(jnp.int32, (ROWS, LANES), 1)
    row = jnp.zeros((ROWS, LANES), jnp.int32)
    for k, number in enumerate(numbers):
        mine[0, k] = number
        row = jnp.where(lane == k, number, row)
    for q in range(orbs - 1):
        plain[q][...] = orbitals[q]
    for r in range(n // ROWS):
        box[:, r * plane : (r + 1) * plane] = orbitals[orbs - 1, r * ROWS : (r + 1) * ROWS, :]
    box[:, n * plane // ROWS :] = row.astype(f32).astype(bf16)


def setup(own, table, mine):
    orbs, n, _ = own.shape
    half = n // 2
    vmem = pl.BlockSpec(memory_space=pltpu.VMEM)
    return pl.pallas_call(
        setup_kernel,
        out_shape=[
            jax.ShapeDtypeStruct((orbs * half * (n + 2 * half), LANES), f32),
            jax.ShapeDtypeStruct((table.shape[0], 2 * LANES), bf16),
            jax.ShapeDtypeStruct((n + half, LANES), f32),
            jax.ShapeDtypeStruct((orbs * half * n, LANES), f32),
        ],
        in_specs=[vmem, vmem, pl.BlockSpec(memory_space=pltpu.SMEM)],
        out_specs=[vmem] * 4,
        compiler_params=pltpu.CompilerParams(vmem_limit_bytes=16 << 20),
        name="setup",
    )(own, table, mine)


def pair_step(name, n, slots, pieces, tasks, last, mine, own, sines, modes, others, total):
    orbs = len(others)
    plane = n * n
    half = n // 2
    pieces = pieces if last else 0
    vmem = pl.BlockSpec(memory_space=pltpu.VMEM)
    smem = pl.BlockSpec(memory_space=pltpu.SMEM)
    held = jax.ShapeDtypeStruct(total.shape, f32)
    rows = half * n
    scratch = [
        pltpu.VMEM((n, plane), bf16),
        pltpu.VMEM((half * (n + 2 * half), LANES), f32),
        pltpu.VMEM((rows, LANES), f32),
        pltpu.VMEM((rows, LANES), f32),
        pltpu.VMEM((rows, LANES), f32),
        pltpu.SMEM(mine.shape, jnp.int32),
    ]
    shapes = held
    if last:
        shapes = jax.ShapeDtypeStruct((orbs, n, plane), bf16)
        if pieces:
            scratch.insert(0, pltpu.VMEM((orbs * n * plane // LANES, LANES), f32))
            shapes = [jax.ShapeDtypeStruct((8, orbs * n * plane // pieces // 8), bf16)] * pieces
        scratch.insert(0, pltpu.VMEM(held.shape, f32))
    return pl.pallas_call(
        functools.partial(pair_kernel, (n, orbs, slots), pieces, tasks, last),
        out_shape=shapes,
        in_specs=[smem] + [vmem] * (4 + orbs),
        out_specs=[vmem] * pieces if pieces else vmem,
        scratch_shapes=scratch,
        input_output_aliases={} if last else {4 + orbs: 0},
        compiler_params=pltpu.CompilerParams(vmem_limit_bytes=32 << 20),
        cost_estimate=pl.CostEstimate(flops=2 * 12 * 3 * n**4, bytes_accessed=4 * n**3 * 4, transcendentals=0),
        name=name,
    )(mine, own, sines, modes, *others, total)


def gather_kernel(n, orbs, member_ref, *refs):
    devices = len(refs) - 3
    out, rows, mixed = refs[devices:]
    tiles = n * n // LANES
    member = member_ref[0]
    for k in range(devices):
        at = pl.multiple_of(jnp.bitwise_xor(member, k) * 8, 8)
        for t in range(tiles * 3 // 2):
            rows[pl.ds(t * devices * 8 + at, 8), :] = refs[k][:, t * LANES : (t + 1) * LANES].astype(f32)
    for x in range(n // devices):
        for t in range(tiles):
            here = slice((x * tiles + t) * LANES, (x * tiles + t + 1) * LANES)
            at = (x * tiles + t) * orbs * devices
            for a in range(orbs):
                q = x * orbs + a
                tile = t
                if q >= 8:
                    q += 4 * (t * 2 // tiles) - 8
                    tile = tiles + t % (tiles // 2)
                mixed[pl.ds(at + a, devices, stride=orbs), :] = rows[
                    pl.ds(tile * devices * 8 + q, devices, stride=8), :
                ]
            out[:, here] = mixed[at : at + orbs * devices, :]


def body(orbitals, offsets, pick, pair_local, pair_source, pair_count):
    orbs, n, plane = orbitals.shape
    groups = lax.axis_size("grp")
    devices = lax.axis_size("dev")
    member = lax.axis_index("dev").astype(jnp.int32)
    slots = pair_local.shape[2]
    vmem = pl.BlockSpec(memory_space=pltpu.VMEM)
    smem = pl.BlockSpec(memory_space=pltpu.SMEM)
    table = jnp.asarray(np_tables(n))
    numbers = 3 * orbs + 2 * slots + 3 + groups
    *held, mine = pl.pallas_call(
        functools.partial(pack_kernel, groups),
        out_shape=[jax.ShapeDtypeStruct((n, plane), bf16)] * (orbs - 1)
        + [
            jax.ShapeDtypeStruct((ROWS, n * plane // ROWS + LANES), bf16),
            jax.ShapeDtypeStruct((1, numbers), jnp.int32),
        ],
        in_specs=[smem] * 4 + [vmem] * 2,
        out_specs=[vmem] * orbs + [smem],
        name="pack",
    )(offsets, pick.transpose(0, 2, 1), pair_local, pair_source, pair_count, orbitals)
    by_pieces = devices & (devices - 1) == 0 and n % devices == 0 and n // devices * orbs == 12
    pieces = devices if by_pieces else 0
    ring = [(g, (g + 1) % groups) for g in range(groups)]
    own, sines, modes, total = setup(orbitals, table, mine)
    early = [total] * orbs
    for step in range(1, groups):
        last = step == groups - 1
        held = [lax.ppermute(h, "grp", ring) for h in held]
        for q in range(orbs):
            held[q], _ = lax.optimization_barrier((held[q], early[q]))
        early = []
        for tasks in [(True, False)] if last else [(True,), (False,)]:
            name = f"pairs_{step}_{len(early)}"
            total = pair_step(name, n, slots, pieces, tasks, last, mine, own, sines, modes, held, total)
            early.insert(0, total)
        early = [early[0]] * (orbs - 1) + early[-1:]
    if not pieces:
        whole = total.reshape(orbs, n * plane)
        return lax.all_to_all(whole, "dev", split_axis=1, concat_axis=0, tiled=True).astype(f32)
    arrived = [total[0]]
    for k in range(1, devices):
        arrived.append(lax.ppermute(total[k], "dev", [(d, d ^ k) for d in range(devices)]))
    return pl.pallas_call(
        functools.partial(gather_kernel, n, orbs),
        out_shape=jax.ShapeDtypeStruct((orbs * devices, n * plane // devices), f32),
        in_specs=[smem] + [vmem] * devices,
        out_specs=vmem,
        scratch_shapes=[pltpu.VMEM((orbs * n * plane // LANES, LANES), f32)] * 2,
        compiler_params=pltpu.CompilerParams(vmem_limit_bytes=32 << 20),
        name="cells",
    )(member.reshape(1), *arrived)


def solution(mesh):
    return jax.shard_map(
        body,
        mesh=mesh,
        in_specs=(
            P(("grp", "dev"), None, None),
            P(("grp", "dev"), None),
            P("grp", None, None),
            P("grp", "dev", None),
            P("grp", "dev", None),
            P("grp", "dev", None),
        ),
        out_specs=P("grp", "dev"),
        check_vma=False,
    )
```

```python
import functools
import math

import numpy as np

import jax
import jax.numpy as jnp
from jax import lax
from jax.experimental import pallas as pl
from jax.experimental.pallas import tpu as pltpu
from jax.sharding import PartitionSpec as P

LANES = 128
HALF = 64
ROWS = 16
f32 = jnp.float32
bf16 = jnp.bfloat16


def np_tables(n):
    freq = np.arange(n)
    step = math.pi / (n + 1)
    sine = math.sqrt(2.0 / (n + 1)) * np.sin(step * ((freq[:, None] + 1) * (freq[None, :] + 1) % (2 * (n + 1))))
    sine = sine.astype(np.float32)
    high = sine.astype(jnp.bfloat16)
    low = (sine - high.astype(np.float32)).astype(jnp.bfloat16)

    def two(block):
        out = np.zeros((LANES, LANES), jnp.bfloat16)
        out[:n, :n] = block
        out[HALF : HALF + n, HALF : HALF + n] = block
        return out

    lane_side = np.block([[two(high), two(low)], [two(high), two(low)]])
    row_side = np.concatenate([high, high, low, 0 * low], axis=1)
    modes = (2.0 - 2.0 * np.cos(step * (freq + 1.0))).astype(np.float32)
    base = np.ones((n, LANES), np.float32)
    outer = np.ones((n // 2, LANES), np.float32)
    for half in range(2):
        at = half * HALF
        base[:, at : at + n] = modes[:, None] + modes[None, :]
        outer[:, at : at + HALF] = modes[half * (n // 2) : (half + 1) * (n // 2), None]
    pad = np.zeros((n, 2 * LANES - 4 * n), jnp.bfloat16)
    sines = np.concatenate([lane_side, np.concatenate([row_side, pad], axis=1)]).astype(np.float32)
    modes = np.concatenate([base, outer])
    modes = np.pad(modes, ((0, len(sines) - len(modes)), (0, 0)))
    return np.concatenate([sines, modes], axis=1)


def split(x):
    high = x.astype(bf16)
    return high, (x - high.astype(f32)).astype(bf16)


def lane_turn(x, lane_side):
    both = jnp.concatenate(split(x), axis=1)
    out = jnp.dot(both, lane_side, preferred_element_type=f32)
    return out[:, :LANES] + out[:, LANES:]


def row_turn(tiles, row_side):
    columns = []
    for tile in tiles:
        high, low = split(tile)
        columns.append(jnp.concatenate([high, low, high], axis=0))
    out = jnp.dot(row_side, jnp.concatenate(columns, axis=1), preferred_element_type=f32)
    return [out[:, k * LANES : (k + 1) * LANES] for k in range(len(tiles))]


def unpack(dense, put):
    n = dense.shape[0]
    half = n // 2
    lane = lax.broadcasted_iota(jnp.int32, (n, LANES), 1)
    for yo in range(half):
        start = yo * n % LANES
        halves = []
        for h in range(2):
            t = (yo * n // LANES + h * (half * n // LANES)) * LANES
            piece = dense[:, t : t + LANES].astype(f32)
            if start + n > LANES:
                after = dense[:, t + LANES : t + 2 * LANES].astype(f32)
                piece = jnp.where(lane >= start, piece, after)
            amount = (h * HALF - start) % LANES
            halves.append(pltpu.roll(piece, amount, 1) if amount else piece)
        put(yo, jnp.where(lane < HALF, halves[0], halves[1]))


def setup_kernel(own, table, mine, held, sines, modes, total):
    orbs, n, _ = own.shape
    half = n // 2
    wide = n + 2 * half
    for q in range(orbs):

        def put(yo, tile, q=q):
            at = (q * half + yo) * wide + half
            held[at : at + n, :] = tile

        unpack(own.at[q], put)
    sines[...] = table[:, : 2 * LANES].astype(bf16)
    modes[...] = table[: modes.shape[0], 2 * LANES :]
    total[...] = jnp.zeros_like(total)


def pair_kernel(sizes, pieces, tasks, last, *refs):
    n, orbs, slots = sizes
    half = n // 2
    cells_tile = half * n // LANES
    wide = n + 2 * half
    mine, own, sines, modes = refs[:4]
    others = refs[4 : 4 + orbs]
    total_in = refs[4 + orbs]
    rest = list(refs[5 + orbs :])
    if last:
        outs = [rest.pop(0) for _ in range(max(pieces, 1))]
        total = rest.pop(0)
        flat = rest.pop(0) if pieces else None
    else:
        total = rest.pop(0)
    dense, held, moved, field, other, theirs = rest
    lists = others[-1][:, n * n * n // ROWS :].astype(f32).astype(jnp.int32)
    for k in range(mine.shape[1]):
        theirs[0, k] = lists[0, k]

    def fetch(q):
        if q < orbs - 1:
            dense[...] = others[q][...]
        else:
            for r in range(n // ROWS):
                dense[r * ROWS : (r + 1) * ROWS, :] = others[q][:, r * n * n : (r + 1) * n * n]

    lane = lax.broadcasted_iota(jnp.int32, (n, LANES), 1)
    row = lax.broadcasted_iota(jnp.int32, (n, LANES), 0)
    left_half = lane[:half] < HALF
    total[...] = total_in[...]

    at_source = 3 * orbs + slots
    at_count = at_source + slots
    at_group = at_count + 1
    at_pick = at_group + 2
    member = mine[0, at_group + 1]

    def tile_at(base, yo):
        return pl.ds(base + yo * wide + half, n)

    def shifted(ref, base, gap, use):
        gap_x, gap_y, gap_z = gap
        z_at = lax.rem(lane, HALF)
        inside = (
            (z_at < n)
            & (z_at + gap_z >= 0)
            & (z_at + gap_z < n)
            & (row + gap_x >= 0)
            & (row + gap_x < n)
        )
        for yo in range(half):
            s = gap_y + yo
            under = s < 0
            over = s >= half
            src = s + jnp.where(under, half, 0) - jnp.where(over, half, 0)
            tile = ref[pl.ds(base + src * wide + half + gap_x, n), :]
            amount = (2 * LANES - gap_z + jnp.where(under | over, HALF, 0)) % LANES
            tile = pltpu.roll(tile, amount, 1)
            low_lane = jnp.where(under, HALF, 0)
            high_lane = jnp.where(over, HALF, LANES)
            good = inside & (lane >= low_lane) & (lane < high_lane)
            use(yo, jnp.where(good, tile, 0.0))

    def swapped(ref, at):
        a = ref[pl.ds(at, half, stride=n), :]
        b = ref[pl.ds(at + half, half, stride=n), :]
        top = jnp.where(left_half, a, pltpu.roll(b, HALF, 1))
        bottom = jnp.where(left_half, pltpu.roll(a, HALF, 1), b)
        return jnp.concatenate([top, bottom], axis=0)

    def rows_of(ref, at):
        return ref[at * n : (at + 1) * n, :]

    def task(outgoing):
        lister, source = (mine, theirs) if outgoing else (theirs, mine)
        source_group = source[0, at_group]
        listed = lister[0, at_count]
        i_at = jnp.int32(0)
        found = jnp.int32(0)
        for p in range(slots):
            hit = (lister[0, at_source + p] == source_group) & (p < listed)
            i_at = jnp.where(hit, lister[0, 3 * orbs + p], i_at)
            found = jnp.where(hit, 1, found)
        j_at = source[0, at_pick + lister[0, at_group]]
        gap = [lister[0, i_at * 3 + k] - source[0, j_at * 3 + k] for k in range(3)]
        own_at, other_at = (i_at, j_at) if outgoing else (j_at, i_at)
        base = own_at * (half * wide)
        box_i, base_i, box_j, base_j = (own, base, held, 0) if outgoing else (held, 0, own, base)

        @pl.when(found == 1)
        def _():
            for q in range(orbs):
                @pl.when(other_at == q)
                def _():
                    fetch(q)

            def put(yo, tile):
                held[tile_at(0, yo), :] = tile

            unpack(dense, put)

            def use_moved(yo, tile):
                moved[yo * n : (yo + 1) * n, :] = tile
                field[yo * n : (yo + 1) * n, :] = box_i[tile_at(base_i, yo), :] * tile

            shifted(box_j, base_j, gap, use_moved)
            lane_side = sines[: 2 * LANES, :]
            row_side = sines[2 * LANES :, : 3 * n]
            other[...] = lane_turn(field[...], lane_side)
            tiles = row_turn([rows_of(other, at) for at in range(half)], row_side)
            for at in range(half):
                field[at * n : (at + 1) * n, :] = tiles[at]
            tiles = row_turn([swapped(field, at) for at in range(half)], row_side)
            tiles = [tiles[at] / (modes[:n, :] + modes[n + at : n + at + 1, :]) for at in range(half)]
            tiles = row_turn(tiles, row_side)
            for at in range(half):
                other[at * n : (at + 1) * n, :] = tiles[at]
            tiles = row_turn([swapped(other, at) for at in range(half)], row_side)
            for at in range(half):
                field[at * n : (at + 1) * n, :] = tiles[at]
            field[...] = lane_turn(field[...], lane_side)

            if outgoing:
                for yo in range(half):
                    there = pl.ds(own_at * (half * n) + yo * n, n)
                    total[there, :] += rows_of(field, yo) * rows_of(moved, yo)
            else:
                for yo in range(half):
                    term = rows_of(field, yo) * held[tile_at(0, yo), :]
                    held[tile_at(0, yo), :] = term.astype(bf16).astype(f32)

                def add_back(yo, tile):
                    there = pl.ds(own_at * (half * n) + yo * n, n)
                    total[there, :] += tile

                shifted(held, 0, [-k for k in gap], add_back)

    for outgoing in tasks:
        task(outgoing)

    if last:
        for a in range(orbs):
            current = {}
            for yo in range(half):
                start = yo * n % LANES
                first_tile = yo * n // LANES
                tile = total[a * half * n + yo * n : a * half * n + (yo + 1) * n, :]
                for h in range(2):
                    t = first_tile + h * cells_tile
                    amount = (start - h * HALF) % LANES
                    piece = pltpu.roll(tile, amount, 1) if amount else tile
                    current[t] = jnp.where(lane >= start, piece, current[t]) if t in current else piece
                    if start + n >= LANES:
                        here = slice(t * LANES, (t + 1) * LANES)
                        if pieces:
                            flat[pl.ds(t * orbs * n + a, n, stride=orbs), :] = current.pop(t)
                        else:
                            outs[0][a, :, here] = current.pop(t).astype(bf16)
                        if start + n > LANES:
                            current[t + 1] = piece
        depth = n // pieces * orbs if pieces else 0
        tiles = n * n // LANES
        for k in range(pieces):
            at = jnp.bitwise_xor(member, k) * depth
            for t in range(tiles):
                outs[k][:, t * LANES : (t + 1) * LANES] = flat[pl.ds(t * orbs * n + at, 8), :].astype(bf16)
            for t in range(tiles // 2):
                tail = [flat[pl.ds((t + h * tiles // 2) * orbs * n + at + 8, 4), :] for h in range(2)]
                tail_at = (tiles + t) * LANES
                outs[k][:, tail_at : tail_at + LANES] = jnp.concatenate(tail, axis=0).astype(bf16)


def pack_kernel(groups, offsets, pick, pair_local, pair_source, pair_count, orbitals, *outs):
    box, mine = outs
    _, n, plane = orbitals.shape
    orbs = offsets.shape[0]
    group = lax.axis_index("grp").astype(jnp.int32)
    member = lax.axis_index("dev").astype(jnp.int32)
    slots = pair_local.shape[2]
    numbers = [offsets[a, k] for a in range(orbs) for k in range(3)]
    numbers += [pair_local[0, 0, p] for p in range(slots)]
    numbers += [pair_source[0, 0, p] for p in range(slots)]
    numbers += [pair_count[0, 0, 0], group, member]
    numbers += [pick[0, g, member] for g in range(groups)]
    lane = lax.broadcasted_iota(jnp.int32, (ROWS, LANES), 1)
    row = jnp.zeros((ROWS, LANES), jnp.int32)
    for k, number in enumerate(numbers):
        mine[0, k] = number
        row = jnp.where(lane == k, number, row)
    for r in range(n // ROWS):
        box[:, r * plane : (r + 1) * plane] = orbitals[0, r * ROWS : (r + 1) * ROWS, :]
    box[:, n * plane // ROWS :] = row.astype(f32).astype(bf16)


def setup(own, table, mine):
    orbs, n, _ = own.shape
    half = n // 2
    vmem = pl.BlockSpec(memory_space=pltpu.VMEM)
    return pl.pallas_call(
        setup_kernel,
        out_shape=[
            jax.ShapeDtypeStruct((orbs * half * (n + 2 * half), LANES), f32),
            jax.ShapeDtypeStruct((table.shape[0], 2 * LANES), bf16),
            jax.ShapeDtypeStruct((n + half, LANES), f32),
            jax.ShapeDtypeStruct((orbs * half * n, LANES), f32),
        ],
        in_specs=[vmem, vmem, pl.BlockSpec(memory_space=pltpu.SMEM)],
        out_specs=[vmem] * 4,
        compiler_params=pltpu.CompilerParams(vmem_limit_bytes=16 << 20),
        name="setup",
    )(own, table, mine)


def pair_step(name, n, slots, pieces, tasks, last, mine, own, sines, modes, others, total):
    orbs = len(others)
    plane = n * n
    half = n // 2
    pieces = pieces if last else 0
    vmem = pl.BlockSpec(memory_space=pltpu.VMEM)
    smem = pl.BlockSpec(memory_space=pltpu.SMEM)
    held = jax.ShapeDtypeStruct(total.shape, f32)
    rows = half * n
    scratch = [
        pltpu.VMEM((n, plane), bf16),
        pltpu.VMEM((half * (n + 2 * half), LANES), f32),
        pltpu.VMEM((rows, LANES), f32),
        pltpu.VMEM((rows, LANES), f32),
        pltpu.VMEM((rows, LANES), f32),
        pltpu.SMEM(mine.shape, jnp.int32),
    ]
    shapes = held
    if last:
        shapes = jax.ShapeDtypeStruct((orbs, n, plane), bf16)
        if pieces:
            scratch.insert(0, pltpu.VMEM((orbs * n * plane // LANES, LANES), f32))
            shapes = [jax.ShapeDtypeStruct((8, orbs * n * plane // pieces // 8), bf16)] * pieces
        scratch.insert(0, pltpu.VMEM(held.shape, f32))
    return pl.pallas_call(
        functools.partial(pair_kernel, (n, orbs, slots), pieces, tasks, last),
        out_shape=shapes,
        in_specs=[smem] + [vmem] * (4 + orbs),
        out_specs=[vmem] * pieces if pieces else vmem,
        scratch_shapes=scratch,
        input_output_aliases={} if last else {4 + orbs: 0},
        compiler_params=pltpu.CompilerParams(vmem_limit_bytes=32 << 20),
        cost_estimate=pl.CostEstimate(flops=2 * 12 * 3 * n**4, bytes_accessed=4 * n**3 * 4, transcendentals=0),
        name=name,
    )(mine, own, sines, modes, *others, total)


def gather_kernel(n, orbs, member_ref, *refs):
    devices = len(refs) - 3
    out, rows, mixed = refs[devices:]
    tiles = n * n // LANES
    member = member_ref[0]
    for k in range(devices):
        at = pl.multiple_of(jnp.bitwise_xor(member, k) * 8, 8)
        for t in range(tiles * 3 // 2):
            rows[pl.ds(t * devices * 8 + at, 8), :] = refs[k][:, t * LANES : (t + 1) * LANES].astype(f32)
    for x in range(n // devices):
        for t in range(tiles):
            here = slice((x * tiles + t) * LANES, (x * tiles + t + 1) * LANES)
            at = (x * tiles + t) * orbs * devices
            for a in range(orbs):
                q = x * orbs + a
                tile = t
                if q >= 8:
                    q += 4 * (t * 2 // tiles) - 8
                    tile = tiles + t % (tiles // 2)
                mixed[pl.ds(at + a, devices, stride=orbs), :] = rows[
                    pl.ds(tile * devices * 8 + q, devices, stride=8), :
                ]
            out[:, here] = mixed[at : at + orbs * devices, :]


def body(orbitals, offsets, pick, pair_local, pair_source, pair_count):
    orbs, n, plane = orbitals.shape
    groups = lax.axis_size("grp")
    devices = lax.axis_size("dev")
    member = lax.axis_index("dev").astype(jnp.int32)
    slots = pair_local.shape[2]
    vmem = pl.BlockSpec(memory_space=pltpu.VMEM)
    smem = pl.BlockSpec(memory_space=pltpu.SMEM)
    table = jnp.asarray(np_tables(n))
    numbers = 3 * orbs + 2 * slots + 3 + groups
    last_box, mine = pl.pallas_call(
        functools.partial(pack_kernel, groups),
        grid=(1,),
        out_shape=[
            jax.ShapeDtypeStruct((ROWS, n * plane // ROWS + LANES), bf16),
            jax.ShapeDtypeStruct((1, numbers), jnp.int32),
        ],
        in_specs=[smem] * 4 + [vmem, pl.BlockSpec((1, n, plane), lambda i: (orbs - 1, 0, 0))],
        out_specs=[vmem, smem],
        name="pack",
    )(offsets, pick.transpose(0, 2, 1), pair_local, pair_source, pair_count, orbitals)
    held = [orbitals[q] for q in range(orbs - 1)] + [last_box]
    by_pieces = devices & (devices - 1) == 0 and n % devices == 0 and n // devices * orbs == 12
    pieces = devices if by_pieces else 0
    ring = [(g, (g + 1) % groups) for g in range(groups)]
    own, sines, modes, total = setup(orbitals, table, mine)
    early = [total] * orbs
    for step in range(1, groups):
        last = step == groups - 1
        held = [lax.ppermute(h, "grp", ring) for h in held]
        for q in range(orbs):
            held[q], _ = lax.optimization_barrier((held[q], early[q]))
        early = []
        for tasks in [(True, False)] if last else [(True,), (False,)]:
            name = f"pairs_{step}_{len(early)}"
            total = pair_step(name, n, slots, pieces, tasks, last, mine, own, sines, modes, held, total)
            early.insert(0, total)
        early = early[-1:] * (orbs - 1) + [early[0]]
    if not pieces:
        whole = total.reshape(orbs, n * plane)
        return lax.all_to_all(whole, "dev", split_axis=1, concat_axis=0, tiled=True).astype(f32)
    arrived = [total[0]]
    for k in range(1, devices):
        arrived.append(lax.ppermute(total[k], "dev", [(d, d ^ k) for d in range(devices)]))
    return pl.pallas_call(
        functools.partial(gather_kernel, n, orbs),
        out_shape=jax.ShapeDtypeStruct((orbs * devices, n * plane // devices), f32),
        in_specs=[smem] + [vmem] * devices,
        out_specs=vmem,
        scratch_shapes=[pltpu.VMEM((orbs * n * plane // LANES, LANES), f32)] * 2,
        compiler_params=pltpu.CompilerParams(vmem_limit_bytes=32 << 20),
        name="cells",
    )(member.reshape(1), *arrived)


def solution(mesh):
    return jax.shard_map(
        body,
        mesh=mesh,
        in_specs=(
            P(("grp", "dev"), None, None),
            P(("grp", "dev"), None),
            P("grp", None, None),
            P("grp", "dev", None),
            P("grp", "dev", None),
            P("grp", "dev", None),
        ),
        out_specs=P("grp", "dev"),
        check_vma=False,
    )
```

```python
import functools
import math

import numpy as np

import jax
import jax.numpy as jnp
from jax import lax
from jax.experimental import pallas as pl
from jax.experimental.pallas import tpu as pltpu
from jax.sharding import PartitionSpec as P

LANES = 128
HALF = 64
ROWS = 16
f32 = jnp.float32
bf16 = jnp.bfloat16


def np_tables(n):
    freq = np.arange(n)
    step = math.pi / (n + 1)
    sine = math.sqrt(2.0 / (n + 1)) * np.sin(step * ((freq[:, None] + 1) * (freq[None, :] + 1) % (2 * (n + 1))))
    sine = sine.astype(np.float32)
    high = sine.astype(jnp.bfloat16)
    low = (sine - high.astype(np.float32)).astype(jnp.bfloat16)

    def two(block):
        out = np.zeros((LANES, LANES), jnp.bfloat16)
        out[:n, :n] = block
        out[HALF : HALF + n, HALF : HALF + n] = block
        return out

    lane_side = np.block([[two(high), two(low)], [two(high), two(low)]])
    row_side = np.concatenate([high, high, low, 0 * low], axis=1)
    modes = (2.0 - 2.0 * np.cos(step * (freq + 1.0))).astype(np.float32)
    base = np.ones((n, LANES), np.float32)
    outer = np.ones((n // 2, LANES), np.float32)
    for half in range(2):
        at = half * HALF
        base[:, at : at + n] = modes[:, None] + modes[None, :]
        outer[:, at : at + HALF] = modes[half * (n // 2) : (half + 1) * (n // 2), None]
    pad = np.zeros((n, 2 * LANES - 4 * n), jnp.bfloat16)
    sines = np.concatenate([lane_side, np.concatenate([row_side, pad], axis=1)]).astype(np.float32)
    modes = np.concatenate([base, outer])
    modes = np.pad(modes, ((0, len(sines) - len(modes)), (0, 0)))
    return np.concatenate([sines, modes], axis=1)


def split(x):
    high = x.astype(bf16)
    return high, (x - high.astype(f32)).astype(bf16)


def lane_turn(x, lane_side):
    both = jnp.concatenate(split(x), axis=1)
    out = jnp.dot(both, lane_side, preferred_element_type=f32)
    return out[:, :LANES] + out[:, LANES:]


def row_turn(tiles, row_side):
    columns = []
    for tile in tiles:
        high, low = split(tile)
        columns.append(jnp.concatenate([high, low, high], axis=0))
    out = jnp.dot(row_side, jnp.concatenate(columns, axis=1), preferred_element_type=f32)
    return [out[:, k * LANES : (k + 1) * LANES] for k in range(len(tiles))]


def unpack(dense, put):
    n = dense.shape[0]
    half = n // 2
    lane = lax.broadcasted_iota(jnp.int32, (n, LANES), 1)
    for yo in range(half):
        start = yo * n % LANES
        halves = []
        for h in range(2):
            t = (yo * n // LANES + h * (half * n // LANES)) * LANES
            piece = dense[:, t : t + LANES].astype(f32)
            if start + n > LANES:
                after = dense[:, t + LANES : t + 2 * LANES].astype(f32)
                piece = jnp.where(lane >= start, piece, after)
            amount = (h * HALF - start) % LANES
            halves.append(pltpu.roll(piece, amount, 1) if amount else piece)
        put(yo, jnp.where(lane < HALF, halves[0], halves[1]))


def setup_kernel(own, table, mine, held, sines, modes, total):
    orbs, n, _ = own.shape
    half = n // 2
    wide = n + 2 * half
    for q in range(orbs):

        def put(yo, tile, q=q):
            at = (q * half + yo) * wide + half
            held[at : at + n, :] = tile

        unpack(own.at[q], put)
    sines[...] = table[:, : 2 * LANES].astype(bf16)
    modes[...] = table[: modes.shape[0], 2 * LANES :]
    total[...] = jnp.zeros_like(total)


def pair_kernel(sizes, pieces, tasks, last, *refs):
    n, orbs, slots = sizes
    half = n // 2
    cells_tile = half * n // LANES
    wide = n + 2 * half
    mine, own, sines, modes = refs[:4]
    others = refs[4 : 4 + orbs]
    total_in = refs[4 + orbs]
    rest = list(refs[5 + orbs :])
    if last:
        outs = [rest.pop(0) for _ in range(max(pieces, 1))]
        total = rest.pop(0)
        flat = rest.pop(0) if pieces else None
    else:
        total = rest.pop(0)
    dense, held, moved, field, other, theirs = rest
    lists = others[-1][:, n * n * n // ROWS :].astype(f32).astype(jnp.int32)
    for k in range(mine.shape[1]):
        theirs[0, k] = lists[0, k]

    def fetch(q):
        if q < orbs - 1:
            dense[...] = others[q][...]
        else:
            for r in range(n // ROWS):
                dense[r * ROWS : (r + 1) * ROWS, :] = others[q][:, r * n * n : (r + 1) * n * n]

    lane = lax.broadcasted_iota(jnp.int32, (n, LANES), 1)
    row = lax.broadcasted_iota(jnp.int32, (n, LANES), 0)
    left_half = lane[:half] < HALF
    total[...] = total_in[...]

    at_source = 3 * orbs + slots
    at_count = at_source + slots
    at_group = at_count + 1
    at_pick = at_group + 2
    member = mine[0, at_group + 1]

    def tile_at(base, yo):
        return pl.ds(base + yo * wide + half, n)

    def shifted(ref, base, gap, use):
        gap_x, gap_y, gap_z = gap
        z_at = lax.rem(lane, HALF)
        inside = (
            (z_at < n)
            & (z_at + gap_z >= 0)
            & (z_at + gap_z < n)
            & (row + gap_x >= 0)
            & (row + gap_x < n)
        )
        for yo in range(half):
            s = gap_y + yo
            under = s < 0
            over = s >= half
            src = s + jnp.where(under, half, 0) - jnp.where(over, half, 0)
            tile = ref[pl.ds(base + src * wide + half + gap_x, n), :]
            amount = (2 * LANES - gap_z + jnp.where(under | over, HALF, 0)) % LANES
            tile = pltpu.roll(tile, amount, 1)
            low_lane = jnp.where(under, HALF, 0)
            high_lane = jnp.where(over, HALF, LANES)
            good = inside & (lane >= low_lane) & (lane < high_lane)
            use(yo, jnp.where(good, tile, 0.0))

    def swapped(ref, at):
        a = ref[pl.ds(at, half, stride=n), :]
        b = ref[pl.ds(at + half, half, stride=n), :]
        top = jnp.where(left_half, a, pltpu.roll(b, HALF, 1))
        bottom = jnp.where(left_half, pltpu.roll(a, HALF, 1), b)
        return jnp.concatenate([top, bottom], axis=0)

    def rows_of(ref, at):
        return ref[at * n : (at + 1) * n, :]

    def task(outgoing):
        lister, source = (mine, theirs) if outgoing else (theirs, mine)
        source_group = source[0, at_group]
        listed = lister[0, at_count]
        i_at = jnp.int32(0)
        found = jnp.int32(0)
        for p in range(slots):
            hit = (lister[0, at_source + p] == source_group) & (p < listed)
            i_at = jnp.where(hit, lister[0, 3 * orbs + p], i_at)
            found = jnp.where(hit, 1, found)
        j_at = source[0, at_pick + lister[0, at_group]]
        gap = [lister[0, i_at * 3 + k] - source[0, j_at * 3 + k] for k in range(3)]
        own_at, other_at = (i_at, j_at) if outgoing else (j_at, i_at)
        base = own_at * (half * wide)
        box_i, base_i, box_j, base_j = (own, base, held, 0) if outgoing else (held, 0, own, base)

        @pl.when(found == 1)
        def _():
            for q in range(orbs):
                @pl.when(other_at == q)
                def _():
                    fetch(q)

            def put(yo, tile):
                held[tile_at(0, yo), :] = tile

            unpack(dense, put)

            def use_moved(yo, tile):
                moved[yo * n : (yo + 1) * n, :] = tile
                field[yo * n : (yo + 1) * n, :] = box_i[tile_at(base_i, yo), :] * tile

            shifted(box_j, base_j, gap, use_moved)
            lane_side = sines[: 2 * LANES, :]
            row_side = sines[2 * LANES :, : 3 * n]
            other[...] = lane_turn(field[...], lane_side)
            tiles = row_turn([rows_of(other, at) for at in range(half)], row_side)
            for at in range(half):
                field[at * n : (at + 1) * n, :] = tiles[at]
            tiles = row_turn([swapped(field, at) for at in range(half)], row_side)
            tiles = [tiles[at] / (modes[:n, :] + modes[n + at : n + at + 1, :]) for at in range(half)]
            tiles = row_turn(tiles, row_side)
            for at in range(half):
                other[at * n : (at + 1) * n, :] = tiles[at]
            tiles = row_turn([swapped(other, at) for at in range(half)], row_side)
            for at in range(half):
                field[at * n : (at + 1) * n, :] = tiles[at]
            field[...] = lane_turn(field[...], lane_side)

            if outgoing:
                for yo in range(half):
                    there = pl.ds(own_at * (half * n) + yo * n, n)
                    total[there, :] += rows_of(field, yo) * rows_of(moved, yo)
            else:
                for yo in range(half):
                    term = rows_of(field, yo) * held[tile_at(0, yo), :]
                    held[tile_at(0, yo), :] = term.astype(bf16).astype(f32)

                def add_back(yo, tile):
                    there = pl.ds(own_at * (half * n) + yo * n, n)
                    total[there, :] += tile

                shifted(held, 0, [-k for k in gap], add_back)

    for outgoing in tasks:
        task(outgoing)

    if last:
        for a in range(orbs):
            current = {}
            for yo in range(half):
                start = yo * n % LANES
                first_tile = yo * n // LANES
                tile = total[a * half * n + yo * n : a * half * n + (yo + 1) * n, :]
                for h in range(2):
                    t = first_tile + h * cells_tile
                    amount = (start - h * HALF) % LANES
                    piece = pltpu.roll(tile, amount, 1) if amount else tile
                    current[t] = jnp.where(lane >= start, piece, current[t]) if t in current else piece
                    if start + n >= LANES:
                        here = slice(t * LANES, (t + 1) * LANES)
                        if pieces:
                            flat[pl.ds(t * orbs * n + a, n, stride=orbs), :] = current.pop(t)
                        else:
                            outs[0][a, :, here] = current.pop(t).astype(bf16)
                        if start + n > LANES:
                            current[t + 1] = piece
        depth = n // pieces * orbs if pieces else 0
        tiles = n * n // LANES
        for k in range(pieces):
            at = jnp.bitwise_xor(member, k) * depth
            for t in range(tiles):
                outs[k][:, t * LANES : (t + 1) * LANES] = flat[pl.ds(t * orbs * n + at, 8), :].astype(bf16)
            for t in range(tiles // 2):
                tail = [flat[pl.ds((t + h * tiles // 2) * orbs * n + at + 8, 4), :] for h in range(2)]
                tail_at = (tiles + t) * LANES
                outs[k][:, tail_at : tail_at + LANES] = jnp.concatenate(tail, axis=0).astype(bf16)


def pack_kernel(groups, offsets, pick, pair_local, pair_source, pair_count, orbitals, *outs):
    box, mine = outs
    _, n, plane = orbitals.shape
    orbs = offsets.shape[0]
    group = lax.axis_index("grp").astype(jnp.int32)
    member = lax.axis_index("dev").astype(jnp.int32)
    slots = pair_local.shape[2]
    numbers = [offsets[a, k] for a in range(orbs) for k in range(3)]
    numbers += [pair_local[0, 0, p] for p in range(slots)]
    numbers += [pair_source[0, 0, p] for p in range(slots)]
    numbers += [pair_count[0, 0, 0], group, member]
    numbers += [pick[0, g, member] for g in range(groups)]
    lane = lax.broadcasted_iota(jnp.int32, (ROWS, LANES), 1)
    row = jnp.zeros((ROWS, LANES), jnp.int32)
    for k, number in enumerate(numbers):
        mine[0, k] = number
        row = jnp.where(lane == k, number, row)
    for r in range(n // ROWS):
        box[:, r * plane : (r + 1) * plane] = orbitals[0, r * ROWS : (r + 1) * ROWS, :]
    box[:, n * plane // ROWS :] = row.astype(f32).astype(bf16)


def setup(own, table, mine):
    orbs, n, _ = own.shape
    half = n // 2
    vmem = pl.BlockSpec(memory_space=pltpu.VMEM)
    return pl.pallas_call(
        setup_kernel,
        out_shape=[
            jax.ShapeDtypeStruct((orbs * half * (n + 2 * half), LANES), f32),
            jax.ShapeDtypeStruct((table.shape[0], 2 * LANES), bf16),
            jax.ShapeDtypeStruct((n + half, LANES), f32),
            jax.ShapeDtypeStruct((orbs * half * n, LANES), f32),
        ],
        in_specs=[vmem, vmem, pl.BlockSpec(memory_space=pltpu.SMEM)],
        out_specs=[vmem] * 4,
        compiler_params=pltpu.CompilerParams(vmem_limit_bytes=16 << 20),
        name="setup",
    )(own, table, mine)


def pair_step(name, n, slots, pieces, tasks, last, mine, own, sines, modes, others, total):
    orbs = len(others)
    plane = n * n
    half = n // 2
    pieces = pieces if last else 0
    vmem = pl.BlockSpec(memory_space=pltpu.VMEM)
    smem = pl.BlockSpec(memory_space=pltpu.SMEM)
    held = jax.ShapeDtypeStruct(total.shape, f32)
    rows = half * n
    scratch = [
        pltpu.VMEM((n, plane), bf16),
        pltpu.VMEM((half * (n + 2 * half), LANES), f32),
        pltpu.VMEM((rows, LANES), f32),
        pltpu.VMEM((rows, LANES), f32),
        pltpu.VMEM((rows, LANES), f32),
        pltpu.SMEM(mine.shape, jnp.int32),
    ]
    shapes = held
    if last:
        shapes = jax.ShapeDtypeStruct((orbs, n, plane), bf16)
        if pieces:
            scratch.insert(0, pltpu.VMEM((orbs * n * plane // LANES + 8, LANES), f32))
            shapes = [jax.ShapeDtypeStruct((8, orbs * n * plane // pieces // 8), bf16)] * pieces
        scratch.insert(0, pltpu.VMEM(held.shape, f32))
    return pl.pallas_call(
        functools.partial(pair_kernel, (n, orbs, slots), pieces, tasks, last),
        out_shape=shapes,
        in_specs=[smem] + [vmem] * (4 + orbs),
        out_specs=[vmem] * pieces if pieces else vmem,
        scratch_shapes=scratch,
        input_output_aliases={} if last else {4 + orbs: 0},
        compiler_params=pltpu.CompilerParams(vmem_limit_bytes=32 << 20),
        cost_estimate=pl.CostEstimate(flops=2 * 12 * 3 * n**4, bytes_accessed=4 * n**3 * 4, transcendentals=0),
        name=name,
    )(mine, own, sines, modes, *others, total)


def gather_kernel(n, orbs, member_ref, *refs):
    devices = len(refs) - 3
    out, rows, mixed = refs[devices:]
    tiles = n * n // LANES
    member = member_ref[0]
    for k in range(devices):
        at = pl.multiple_of(jnp.bitwise_xor(member, k) * 8, 8)
        for t in range(tiles * 3 // 2):
            rows[pl.ds(t * devices * 8 + at, 8), :] = refs[k][:, t * LANES : (t + 1) * LANES].astype(f32)
    for x in range(n // devices):
        for t in range(tiles):
            here = slice((x * tiles + t) * LANES, (x * tiles + t + 1) * LANES)
            at = (x * tiles + t) * orbs * devices
            for a in range(orbs):
                q = x * orbs + a
                tile = t
                if q >= 8:
                    q += 4 * (t * 2 // tiles) - 8
                    tile = tiles + t % (tiles // 2)
                mixed[pl.ds(at + a, devices, stride=orbs), :] = rows[
                    pl.ds(tile * devices * 8 + q, devices, stride=8), :
                ]
            out[:, here] = mixed[at : at + orbs * devices, :]


def body(orbitals, offsets, pick, pair_local, pair_source, pair_count):
    orbs, n, plane = orbitals.shape
    groups = lax.axis_size("grp")
    devices = lax.axis_size("dev")
    member = lax.axis_index("dev").astype(jnp.int32)
    slots = pair_local.shape[2]
    vmem = pl.BlockSpec(memory_space=pltpu.VMEM)
    smem = pl.BlockSpec(memory_space=pltpu.SMEM)
    table = jnp.asarray(np_tables(n))
    numbers = 3 * orbs + 2 * slots + 3 + groups
    last_box, mine = pl.pallas_call(
        functools.partial(pack_kernel, groups),
        grid=(1,),
        out_shape=[
            jax.ShapeDtypeStruct((ROWS, n * plane // ROWS + LANES), bf16),
            jax.ShapeDtypeStruct((1, numbers), jnp.int32),
        ],
        in_specs=[smem] * 4 + [vmem, pl.BlockSpec((1, n, plane), lambda i: (orbs - 1, 0, 0))],
        out_specs=[vmem, smem],
        name="pack",
    )(offsets, pick.transpose(0, 2, 1), pair_local, pair_source, pair_count, orbitals)
    held = [orbitals[q] for q in range(orbs - 1)] + [last_box]
    by_pieces = devices & (devices - 1) == 0 and n % devices == 0 and n // devices * orbs == 12
    pieces = devices if by_pieces else 0
    ring = [(g, (g + 1) % groups) for g in range(groups)]
    own, sines, modes, total = setup(orbitals, table, mine)
    early = [total] * orbs
    for step in range(1, groups):
        last = step == groups - 1
        held = [lax.ppermute(h, "grp", ring) for h in held]
        for q in range(orbs):
            held[q], _ = lax.optimization_barrier((held[q], early[q]))
        early = []
        for tasks in [(True, False)] if last else [(True,), (False,)]:
            name = f"pairs_{step}_{len(early)}"
            total = pair_step(name, n, slots, pieces, tasks, last, mine, own, sines, modes, held, total)
            early.insert(0, total)
        early = early[-1:] * (orbs - 1) + [early[0]]
    if not pieces:
        whole = total.reshape(orbs, n * plane)
        return lax.all_to_all(whole, "dev", split_axis=1, concat_axis=0, tiled=True).astype(f32)
    arrived = [total[0]]
    for k in range(1, devices):
        arrived.append(lax.ppermute(total[k], "dev", [(d, d ^ k) for d in range(devices)]))
    return pl.pallas_call(
        functools.partial(gather_kernel, n, orbs),
        out_shape=jax.ShapeDtypeStruct((orbs * devices, n * plane // devices), f32),
        in_specs=[smem] + [vmem] * devices,
        out_specs=vmem,
        scratch_shapes=[pltpu.VMEM((orbs * n * plane // LANES, LANES), f32)] * 2,
        compiler_params=pltpu.CompilerParams(vmem_limit_bytes=32 << 20),
        name="cells",
    )(member.reshape(1), *arrived)


def solution(mesh):
    return jax.shard_map(
        body,
        mesh=mesh,
        in_specs=(
            P(("grp", "dev"), None, None),
            P(("grp", "dev"), None),
            P("grp", None, None),
            P("grp", "dev", None),
            P("grp", "dev", None),
            P("grp", "dev", None),
        ),
        out_specs=P("grp", "dev"),
        check_vma=False,
    )
```

```python
import functools
import math

import numpy as np

import jax
import jax.numpy as jnp
from jax import lax
from jax.experimental import pallas as pl
from jax.experimental.pallas import tpu as pltpu
from jax.sharding import PartitionSpec as P

LANES = 128
HALF = 64
ROWS = 16
f32 = jnp.float32
bf16 = jnp.bfloat16


def np_tables(n):
    freq = np.arange(n)
    step = math.pi / (n + 1)
    sine = math.sqrt(2.0 / (n + 1)) * np.sin(step * ((freq[:, None] + 1) * (freq[None, :] + 1) % (2 * (n + 1))))
    sine = sine.astype(np.float32)
    high = sine.astype(jnp.bfloat16)
    low = (sine - high.astype(np.float32)).astype(jnp.bfloat16)

    def two(block):
        out = np.zeros((LANES, LANES), jnp.bfloat16)
        out[:n, :n] = block
        out[HALF : HALF + n, HALF : HALF + n] = block
        return out

    lane_side = np.block([[two(high), two(low)], [two(high), two(low)]])
    row_side = np.concatenate([high, high, low, 0 * low], axis=1)
    modes = (2.0 - 2.0 * np.cos(step * (freq + 1.0))).astype(np.float32)
    base = np.ones((n, LANES), np.float32)
    outer = np.ones((n // 2, LANES), np.float32)
    for half in range(2):
        at = half * HALF
        base[:, at : at + n] = modes[:, None] + modes[None, :]
        outer[:, at : at + HALF] = modes[half * (n // 2) : (half + 1) * (n // 2), None]
    pad = np.zeros((n, 2 * LANES - 4 * n), jnp.bfloat16)
    sines = np.concatenate([lane_side, np.concatenate([row_side, pad], axis=1)]).astype(np.float32)
    modes = np.concatenate([base, outer])
    modes = np.pad(modes, ((0, len(sines) - len(modes)), (0, 0)))
    return np.concatenate([sines, modes], axis=1)


def split(x):
    high = x.astype(bf16)
    return high, (x - high.astype(f32)).astype(bf16)


def lane_turn(x, lane_side):
    both = jnp.concatenate(split(x), axis=1)
    out = jnp.dot(both, lane_side, preferred_element_type=f32)
    return out[:, :LANES] + out[:, LANES:]


def row_turn(tiles, row_side):
    columns = []
    for tile in tiles:
        high, low = split(tile)
        columns.append(jnp.concatenate([high, low, high], axis=0))
    out = jnp.dot(row_side, jnp.concatenate(columns, axis=1), preferred_element_type=f32)
    return [out[:, k * LANES : (k + 1) * LANES] for k in range(len(tiles))]


def unpack(dense, put):
    n = dense.shape[0]
    half = n // 2
    lane = lax.broadcasted_iota(jnp.int32, (n, LANES), 1)
    for yo in range(half):
        start = yo * n % LANES
        halves = []
        for h in range(2):
            t = (yo * n // LANES + h * (half * n // LANES)) * LANES
            piece = dense[:, t : t + LANES].astype(f32)
            if start + n > LANES:
                after = dense[:, t + LANES : t + 2 * LANES].astype(f32)
                piece = jnp.where(lane >= start, piece, after)
            amount = (h * HALF - start) % LANES
            halves.append(pltpu.roll(piece, amount, 1) if amount else piece)
        put(yo, jnp.where(lane < HALF, halves[0], halves[1]))


def setup_kernel(own, table, mine, held, sines, modes, total):
    orbs, n, _ = own.shape
    half = n // 2
    wide = n + 2 * half
    for q in range(orbs):

        def put(yo, tile, q=q):
            at = (q * half + yo) * wide + half
            held[at : at + n, :] = tile

        unpack(own.at[q], put)
    sines[...] = table[:, : 2 * LANES].astype(bf16)
    modes[...] = table[: modes.shape[0], 2 * LANES :]
    total[...] = jnp.zeros_like(total)


def pair_kernel(sizes, pieces, tasks, last, *refs):
    n, orbs, slots = sizes
    half = n // 2
    cells_tile = half * n // LANES
    wide = n + 2 * half
    mine, own, sines, modes = refs[:4]
    others = refs[4 : 4 + orbs]
    total_in = refs[4 + orbs]
    rest = list(refs[5 + orbs :])
    if last:
        outs = [rest.pop(0) for _ in range(max(pieces, 1))]
        total = rest.pop(0)
        flat = rest.pop(0) if pieces else None
    else:
        total = rest.pop(0)
    dense, held, moved, field, other, theirs = rest
    lists = others[-1][:, n * n * n // ROWS :].astype(f32).astype(jnp.int32)
    for k in range(mine.shape[1]):
        theirs[0, k] = lists[0, k]

    def fetch(q):
        if q < orbs - 1:
            dense[...] = others[q][...]
        else:
            for r in range(n // ROWS):
                dense[r * ROWS : (r + 1) * ROWS, :] = others[q][:, r * n * n : (r + 1) * n * n]

    lane = lax.broadcasted_iota(jnp.int32, (n, LANES), 1)
    row = lax.broadcasted_iota(jnp.int32, (n, LANES), 0)
    left_half = lane[:half] < HALF
    total[...] = total_in[...]

    at_source = 3 * orbs + slots
    at_count = at_source + slots
    at_group = at_count + 1
    at_pick = at_group + 2
    member = mine[0, at_group + 1]

    def tile_at(base, yo):
        return pl.ds(base + yo * wide + half, n)

    def shifted(ref, base, gap, use):
        gap_x, gap_y, gap_z = gap
        z_at = lax.rem(lane, HALF)
        inside = (
            (z_at < n)
            & (z_at + gap_z >= 0)
            & (z_at + gap_z < n)
            & (row + gap_x >= 0)
            & (row + gap_x < n)
        )
        for yo in range(half):
            s = gap_y + yo
            under = s < 0
            over = s >= half
            src = s + jnp.where(under, half, 0) - jnp.where(over, half, 0)
            tile = ref[pl.ds(base + src * wide + half + gap_x, n), :]
            amount = (2 * LANES - gap_z + jnp.where(under | over, HALF, 0)) % LANES
            tile = pltpu.roll(tile, amount, 1)
            low_lane = jnp.where(under, HALF, 0)
            high_lane = jnp.where(over, HALF, LANES)
            good = inside & (lane >= low_lane) & (lane < high_lane)
            use(yo, jnp.where(good, tile, 0.0))

    def swapped(ref, at):
        a = ref[pl.ds(at, half, stride=n), :]
        b = ref[pl.ds(at + half, half, stride=n), :]
        top = jnp.where(left_half, a, pltpu.roll(b, HALF, 1))
        bottom = jnp.where(left_half, pltpu.roll(a, HALF, 1), b)
        return jnp.concatenate([top, bottom], axis=0)

    def rows_of(ref, at):
        return ref[at * n : (at + 1) * n, :]

    def task(outgoing):
        lister, source = (mine, theirs) if outgoing else (theirs, mine)
        source_group = source[0, at_group]
        listed = lister[0, at_count]
        i_at = jnp.int32(0)
        found = jnp.int32(0)
        for p in range(slots):
            hit = (lister[0, at_source + p] == source_group) & (p < listed)
            i_at = jnp.where(hit, lister[0, 3 * orbs + p], i_at)
            found = jnp.where(hit, 1, found)
        j_at = source[0, at_pick + lister[0, at_group]]
        gap = [lister[0, i_at * 3 + k] - source[0, j_at * 3 + k] for k in range(3)]
        own_at, other_at = (i_at, j_at) if outgoing else (j_at, i_at)
        base = own_at * (half * wide)
        box_i, base_i, box_j, base_j = (own, base, held, 0) if outgoing else (held, 0, own, base)

        @pl.when(found == 1)
        def _():
            for q in range(orbs):
                @pl.when(other_at == q)
                def _():
                    fetch(q)

            def put(yo, tile):
                held[tile_at(0, yo), :] = tile

            unpack(dense, put)

            def use_moved(yo, tile):
                moved[yo * n : (yo + 1) * n, :] = tile
                field[yo * n : (yo + 1) * n, :] = box_i[tile_at(base_i, yo), :] * tile

            shifted(box_j, base_j, gap, use_moved)
            lane_side = sines[: 2 * LANES, :]
            row_side = sines[2 * LANES :, : 3 * n]
            other[...] = lane_turn(field[...], lane_side)
            tiles = row_turn([rows_of(other, at) for at in range(half)], row_side)
            for at in range(half):
                field[at * n : (at + 1) * n, :] = tiles[at]
            tiles = row_turn([swapped(field, at) for at in range(half)], row_side)
            tiles = [tiles[at] / (modes[:n, :] + modes[n + at : n + at + 1, :]) for at in range(half)]
            tiles = row_turn(tiles, row_side)
            for at in range(half):
                other[at * n : (at + 1) * n, :] = tiles[at]
            tiles = row_turn([swapped(other, at) for at in range(half)], row_side)
            for at in range(half):
                field[at * n : (at + 1) * n, :] = tiles[at]
            field[...] = lane_turn(field[...], lane_side)

            if outgoing:
                for yo in range(half):
                    there = pl.ds(own_at * (half * n) + yo * n, n)
                    total[there, :] += rows_of(field, yo) * rows_of(moved, yo)
            else:
                for yo in range(half):
                    term = rows_of(field, yo) * held[tile_at(0, yo), :]
                    held[tile_at(0, yo), :] = term.astype(bf16).astype(f32)

                def add_back(yo, tile):
                    there = pl.ds(own_at * (half * n) + yo * n, n)
                    total[there, :] += tile

                shifted(held, 0, [-k for k in gap], add_back)

    for outgoing in tasks:
        task(outgoing)

    if last:
        for a in range(orbs):
            current = {}
            for yo in range(half):
                start = yo * n % LANES
                first_tile = yo * n // LANES
                tile = total[a * half * n + yo * n : a * half * n + (yo + 1) * n, :]
                for h in range(2):
                    t = first_tile + h * cells_tile
                    amount = (start - h * HALF) % LANES
                    piece = pltpu.roll(tile, amount, 1) if amount else tile
                    current[t] = jnp.where(lane >= start, piece, current[t]) if t in current else piece
                    if start + n >= LANES:
                        here = slice(t * LANES, (t + 1) * LANES)
                        if pieces:
                            flat[pl.ds(t * orbs * n + a, n, stride=orbs), :] = current.pop(t)
                        else:
                            outs[0][a, :, here] = current.pop(t).astype(bf16)
                        if start + n > LANES:
                            current[t + 1] = piece
        depth = n // pieces * orbs if pieces else 0
        tiles = n * n // LANES
        for k in range(pieces):
            at = jnp.bitwise_xor(member, k) * depth
            for t in range(tiles):
                outs[k][:, t * LANES : (t + 1) * LANES] = flat[pl.ds(t * orbs * n + at, 8), :].astype(bf16)
            for t in range(tiles // 2):
                tail = [flat[pl.ds((t + h * tiles // 2) * orbs * n + at + 8, 4), :] for h in range(2)]
                tail_at = (tiles + t) * LANES
                outs[k][:, tail_at : tail_at + LANES] = jnp.concatenate(tail, axis=0).astype(bf16)


def pack_kernel(groups, offsets, pick, pair_local, pair_source, pair_count, orbitals, *outs):
    box, mine = outs
    _, n, plane = orbitals.shape
    orbs = offsets.shape[0]
    group = lax.axis_index("grp").astype(jnp.int32)
    member = lax.axis_index("dev").astype(jnp.int32)
    slots = pair_local.shape[2]
    numbers = [offsets[a, k] for a in range(orbs) for k in range(3)]
    numbers += [pair_local[0, 0, p] for p in range(slots)]
    numbers += [pair_source[0, 0, p] for p in range(slots)]
    numbers += [pair_count[0, 0, 0], group, member]
    numbers += [pick[0, g, member] for g in range(groups)]
    lane = lax.broadcasted_iota(jnp.int32, (ROWS, LANES), 1)
    row = jnp.zeros((ROWS, LANES), jnp.int32)
    for k, number in enumerate(numbers):
        mine[0, k] = number
        row = jnp.where(lane == k, number, row)
    for r in range(n // ROWS):
        box[:, r * plane : (r + 1) * plane] = orbitals[0, r * ROWS : (r + 1) * ROWS, :]
    box[:, n * plane // ROWS :] = row.astype(f32).astype(bf16)


def setup(own, table, mine):
    orbs, n, _ = own.shape
    half = n // 2
    vmem = pl.BlockSpec(memory_space=pltpu.VMEM)
    return pl.pallas_call(
        setup_kernel,
        out_shape=[
            jax.ShapeDtypeStruct((orbs * half * (n + 2 * half), LANES), f32),
            jax.ShapeDtypeStruct((table.shape[0], 2 * LANES), bf16),
            jax.ShapeDtypeStruct((n + half, LANES), f32),
            jax.ShapeDtypeStruct((orbs * half * n, LANES), f32),
        ],
        in_specs=[vmem, vmem, pl.BlockSpec(memory_space=pltpu.SMEM)],
        out_specs=[vmem] * 4,
        compiler_params=pltpu.CompilerParams(vmem_limit_bytes=16 << 20),
        name="setup",
    )(own, table, mine)


def pair_step(name, n, slots, pieces, tasks, last, mine, own, sines, modes, others, total):
    orbs = len(others)
    plane = n * n
    half = n // 2
    pieces = pieces if last else 0
    vmem = pl.BlockSpec(memory_space=pltpu.VMEM)
    smem = pl.BlockSpec(memory_space=pltpu.SMEM)
    held = jax.ShapeDtypeStruct(total.shape, f32)
    rows = half * n
    scratch = [
        pltpu.VMEM((n, plane), bf16),
        pltpu.VMEM((half * (n + 2 * half), LANES), f32),
        pltpu.VMEM((rows, LANES), f32),
        pltpu.VMEM((rows, LANES), f32),
        pltpu.VMEM((rows, LANES), f32),
        pltpu.SMEM(mine.shape, jnp.int32),
    ]
    shapes = held
    if last:
        shapes = jax.ShapeDtypeStruct((orbs, n, plane), bf16)
        if pieces:
            scratch.insert(0, pltpu.VMEM((orbs * n * plane // LANES + 8, LANES), f32))
            shapes = [jax.ShapeDtypeStruct((8, orbs * n * plane // pieces // 8), bf16)] * pieces
        scratch.insert(0, pltpu.VMEM(held.shape, f32))
    return pl.pallas_call(
        functools.partial(pair_kernel, (n, orbs, slots), pieces, tasks, last),
        out_shape=shapes,
        in_specs=[smem] + [vmem] * (4 + orbs),
        out_specs=[vmem] * pieces if pieces else vmem,
        scratch_shapes=scratch,
        input_output_aliases={} if last else {4 + orbs: 0},
        compiler_params=pltpu.CompilerParams(vmem_limit_bytes=32 << 20),
        cost_estimate=pl.CostEstimate(flops=2 * 12 * 3 * n**4, bytes_accessed=4 * n**3 * 4, transcendentals=0),
        name=name,
    )(mine, own, sines, modes, *others, total)


def gather_kernel(n, orbs, member_ref, *refs):
    devices = len(refs) - 3
    out, rows, mixed = refs[devices:]
    tiles = n * n // LANES
    member = member_ref[0]
    for k in range(devices):
        at = pl.multiple_of(jnp.bitwise_xor(member, k) * 8, 8)
        for t in range(tiles * 3 // 2):
            rows[pl.ds(t * devices * 8 + at, 8), :] = refs[k][:, t * LANES : (t + 1) * LANES].astype(f32)
    for x in range(n // devices):
        for t in range(tiles):
            here = slice((x * tiles + t) * LANES, (x * tiles + t + 1) * LANES)
            at = (x * tiles + t) * orbs * devices
            for a in range(orbs):
                q = x * orbs + a
                tile = t
                if q >= 8:
                    q += 4 * (t * 2 // tiles) - 8
                    tile = tiles + t % (tiles // 2)
                mixed[pl.ds(at + a, devices, stride=orbs), :] = rows[
                    pl.ds(tile * devices * 8 + q, devices, stride=8), :
                ]
            out[:, here] = mixed[at : at + orbs * devices, :]


def body(orbitals, offsets, pick, pair_local, pair_source, pair_count):
    orbs, n, plane = orbitals.shape
    groups = lax.axis_size("grp")
    devices = lax.axis_size("dev")
    member = lax.axis_index("dev").astype(jnp.int32)
    slots = pair_local.shape[2]
    vmem = pl.BlockSpec(memory_space=pltpu.VMEM)
    smem = pl.BlockSpec(memory_space=pltpu.SMEM)
    table = jnp.asarray(np_tables(n))
    numbers = 3 * orbs + 2 * slots + 3 + groups
    last_box, mine = pl.pallas_call(
        functools.partial(pack_kernel, groups),
        grid=(1,),
        out_shape=[
            jax.ShapeDtypeStruct((ROWS, n * plane // ROWS + LANES), bf16),
            jax.ShapeDtypeStruct((1, numbers), jnp.int32),
        ],
        in_specs=[smem] * 4 + [vmem, pl.BlockSpec((1, n, plane), lambda i: (orbs - 1, 0, 0))],
        out_specs=[vmem, smem],
        name="pack",
    )(offsets, pick.transpose(0, 2, 1), pair_local, pair_source, pair_count, orbitals)
    held = [orbitals[q] for q in range(orbs - 1)] + [last_box]
    by_pieces = devices & (devices - 1) == 0 and n % devices == 0 and n // devices * orbs == 12
    pieces = devices if by_pieces else 0
    ring = [(g, (g + 1) % groups) for g in range(groups)]
    own, sines, modes, total = setup(orbitals, table, mine)
    early = [total] * orbs
    for step in range(1, groups):
        last = step == groups - 1
        held = [lax.ppermute(h, "grp", ring) for h in held]
        for q in range(orbs):
            held[q], _ = lax.optimization_barrier((held[q], early[q]))
        early = []
        for tasks in [(True, False)] if step >= groups - 2 else [(True,), (False,)]:
            name = f"pairs_{step}_{len(early)}"
            total = pair_step(name, n, slots, pieces, tasks, last, mine, own, sines, modes, held, total)
            early.insert(0, total)
        early = early[-1:] * (orbs - 1) + [early[0]]
    if not pieces:
        whole = total.reshape(orbs, n * plane)
        return lax.all_to_all(whole, "dev", split_axis=1, concat_axis=0, tiled=True).astype(f32)
    arrived = [total[0]]
    for k in range(1, devices):
        arrived.append(lax.ppermute(total[k], "dev", [(d, d ^ k) for d in range(devices)]))
    return pl.pallas_call(
        functools.partial(gather_kernel, n, orbs),
        out_shape=jax.ShapeDtypeStruct((orbs * devices, n * plane // devices), f32),
        in_specs=[smem] + [vmem] * devices,
        out_specs=vmem,
        scratch_shapes=[pltpu.VMEM((orbs * n * plane // LANES, LANES), f32)] * 2,
        compiler_params=pltpu.CompilerParams(vmem_limit_bytes=32 << 20),
        name="cells",
    )(member.reshape(1), *arrived)


def solution(mesh):
    return jax.shard_map(
        body,
        mesh=mesh,
        in_specs=(
            P(("grp", "dev"), None, None),
            P(("grp", "dev"), None),
            P("grp", None, None),
            P("grp", "dev", None),
            P("grp", "dev", None),
            P("grp", "dev", None),
        ),
        out_specs=P("grp", "dev"),
        check_vma=False,
    )
```
